128 devices in a mesh: row: 4 (over y), col: 32 (over z, x, core).
Axes of the slice: x: 4, y: 4, z: 4, core: 2. Of those that a mesh axis runs over, the one named last changes fastest.
Arguments:
- tokens: bfloat16 [1536, 6144], P('row', 'col'), may hold values from -6 to 6
- norm_gain: bfloat16 [6144], P('col'), may hold values from 0.36 to 2.7
- inner_weight: bfloat16 [6144, 12288], P('row', 'col'), may hold values from -0.15625 to 0.15625
- outer_weight: bfloat16 [12288, 6144], P('col', 'row'), may hold values from -0.109375 to 0.109375
- cotangent: bfloat16 [1536, 6144], P('row', 'col'), may hold values from -6 to 6
Outputs:
- branch_out: bfloat16 [1536, 6144], P('row', 'col')
- grad_tokens: bfloat16 [1536, 6144], P('row', 'col')
- grad_gain: float32 [6144], P('col')
- grad_inner: float32 [6144, 12288], P('row', 'col')
- grad_outer: float32 [12288, 6144], P('col', 'row')
The draws below stay inside these ranges and needn't reach their ends.
All inputs are finite; a program needn't handle non-finite values.
Results may differ from the reference program's by a relative error of at most 0.0058.
Values may be sent and summed in bfloat16 or wider, within the bound.
A program may use at most 192 MiB of HBM per device.

```python
import jax
import jax.numpy as jnp
from jax import lax

D = 6144
FF = 12288
TOKENS = 1536


def draw_norm_gain(key, part):
    key = jax.random.fold_in(key, 5)
    position = jnp.arange(D, dtype=jnp.float32) / D
    ramp = 0.6 + 1.2 * position
    factor = jax.random.uniform(key, (D,), jnp.float32, 0.8, 1.25)
    return (ramp * factor).astype(jnp.bfloat16)


def spiked(drawn, rng, source, target, parts, factor):
    def block_of(axis_at):
        return (jnp.arange(drawn.shape[axis_at]) // (drawn.shape[axis_at] // parts)).reshape((-1,) + (1,) * (drawn.ndim - 1 - axis_at))

    one_side = jax.random.permutation(rng, parts)[block_of(target)]
    other_side = (block_of(target) + parts // 2) % parts
    return jnp.where((block_of(source) == one_side) | (block_of(source) == other_side), factor * drawn, drawn)


def steps_of(own_key, shape, pieces, low, high):
    loudness, own = 1.0, jax.random.fold_in(own_key, 6)
    for axis_at, blocks in pieces:
        steps = jnp.exp(jax.random.uniform(jax.random.fold_in(own, axis_at), (blocks,), jnp.float32, low / len(pieces), high / len(pieces)))
        loudness = loudness * jnp.repeat(steps, shape[axis_at] // blocks).reshape([-1 if axis == axis_at else 1 for axis in range(len(shape))])
    return loudness


def scatter_about(rng, shape, deviation, bound, split=(), kind=jnp.bfloat16):
    drawn = jax.random.normal(rng, shape, jnp.float32) * deviation
    if len(split) > 0:
        drawn = steps_of(rng, shape, split, -0.22, 0.18) * drawn
    return jnp.clip(drawn, min=-bound, max=bound).astype(kind)


def gaussian_with(rng, extent, scale, most, pieces, heavy, kind=jnp.bfloat16):
    entries = scale * jax.random.normal(rng, extent, jnp.float32)
    if pieces:
        entries = entries * steps_of(rng, extent, pieces, -0.22, 0.18)
    return jnp.clip(spiked(entries, jax.random.fold_in(rng, 3), *heavy), -most, most).astype(kind)


def setup_inputs(seed: int = 0) -> dict:
    splits = jax.random.split(jax.random.key(seed), 6)
    return {
        "tokens": scatter_about(splits[0], (TOKENS, D), 1.0, 6.0, ((0, 4), (1, 32))),
        "norm_gain": draw_norm_gain(jax.random.fold_in(splits[5], 71), 0),
        "inner_weight": gaussian_with(splits[2], (D, FF), D ** -0.5, 0.15625, ((0, 4), (1, 32)), (1, 0, 32, 2.75)),
        "outer_weight": gaussian_with(splits[3], (FF, D), FF ** -0.5, 0.109375, ((0, 32), (1, 4)), (0, 1, 32, 2.75)),
        "cotangent": gaussian_with(splits[4], (TOKENS, D), 1.0, 6.0, ((0, 4), (1, 32)), (0, 1, 32, 2.75)),
    }


inv_sqrt_two = 0.7071067811865476
inv_sqrt_tau = 0.3989422804014327

def gelu_parts(hidden_pre):
    cumulative = 0.5 * (1.0 + lax.erf(hidden_pre * inv_sqrt_two))
    density = jnp.exp(-0.5 * hidden_pre * hidden_pre) * inv_sqrt_tau
    return (hidden_pre * cumulative, cumulative + hidden_pre * density)

def reference(tokens, norm_gain, inner_weight, outer_weight, cotangent):
    values = tokens.astype(jnp.float32)
    row_mean = lax.optimization_barrier(jnp.mean(values, axis=1, keepdims=True))
    centred = values - row_mean
    variance = lax.optimization_barrier(jnp.mean(centred * centred, axis=1, keepdims=True))
    inv_std = lax.rsqrt(variance + 1e-06)
    unit_rows = centred * inv_std
    gain_values = norm_gain.astype(jnp.float32)
    normed = (unit_rows * gain_values).astype(jnp.bfloat16)
    hidden_pre = jnp.dot(normed, inner_weight, preferred_element_type=jnp.float32)
    gelu_value, gelu_slope = gelu_parts(hidden_pre)
    activated = gelu_value.astype(jnp.bfloat16)
    branch_out = jnp.dot(activated, outer_weight, preferred_element_type=jnp.float32).astype(jnp.bfloat16)
    grad_act = jnp.dot(cotangent, outer_weight.T, preferred_element_type=jnp.float32)
    grad_pre = (grad_act * gelu_slope).astype(jnp.bfloat16)
    grad_outer = jnp.dot(activated.T, cotangent, preferred_element_type=jnp.float32)
    grad_inner = jnp.dot(normed.T, grad_pre, preferred_element_type=jnp.float32)
    grad_normed = jnp.dot(grad_pre, inner_weight.T, preferred_element_type=jnp.float32)
    grad_gain = lax.optimization_barrier(jnp.sum(grad_normed * unit_rows, axis=0))
    grad_hat = grad_normed * gain_values
    first_mean = lax.optimization_barrier(jnp.mean(grad_hat, axis=1, keepdims=True))
    second_mean = lax.optimization_barrier(jnp.mean(grad_hat * unit_rows, axis=1, keepdims=True))
    grad_tokens = (inv_std * (grad_hat - first_mean - unit_rows * second_mean)).astype(jnp.bfloat16)
    return (branch_out, grad_tokens, grad_gain, grad_inner, grad_outer)
```

```python
import jax
import jax.numpy as jnp
from jax import lax
from jax.sharding import PartitionSpec as P

inv_sqrt_two = 0.7071067811865476
inv_sqrt_tau = 0.3989422804014327
ROWS = 4
SHARES = 8


def gelu_parts(hidden_pre):
    cumulative = 0.5 * (1.0 + lax.erf(hidden_pre * inv_sqrt_two))
    density = jnp.exp(-0.5 * hidden_pre * hidden_pre) * inv_sqrt_tau
    return (hidden_pre * cumulative, cumulative + hidden_pre * density)


def contract_rows(left, right):
    return lax.dot_general(
        left, right, (((0,), (0,)), ((), ())), preferred_element_type=jnp.float32
    )


def contract_cols(left, right):
    return lax.dot_general(
        left, right, (((1,), (1,)), ((), ())), preferred_element_type=jnp.float32
    )


def swap_pairs():
    pairs = []
    for y in range(ROWS):
        for z in range(ROWS):
            for s in range(SHARES):
                pairs.append((y * 32 + z * 8 + s, z * 32 + y * 8 + s))
    return pairs


def swap(share):
    return lax.ppermute(share, ("row", "col"), swap_pairs())


def chunk_of(share):
    rows, width = share.shape
    pieces = lax.all_gather(swap(share), "col", axis=0)
    pieces = pieces.reshape(ROWS, SHARES, rows, width)
    return pieces.transpose(0, 2, 1, 3).reshape(ROWS * rows, SHARES * width)


def share_of(partial):
    rows, width = partial.shape[0] // ROWS, partial.shape[1] // SHARES
    pieces = partial.reshape(ROWS, rows, SHARES, width).transpose(0, 2, 1, 3)
    pieces = pieces.reshape(ROWS * SHARES, rows, width).astype(jnp.bfloat16)
    summed = lax.psum_scatter(pieces, "col", scatter_dimension=0)
    return swap(summed).astype(jnp.float32)


def body(tokens, norm_gain, inner_weight, outer_weight, cotangent):
    width = tokens.shape[1]
    features = width * 32
    cot_chunk = chunk_of(cotangent)
    values = tokens.astype(jnp.float32)
    own_mean = jnp.mean(values, axis=1, keepdims=True)
    own_second = jnp.sum((values - own_mean) ** 2, axis=1, keepdims=True)
    stats = lax.all_gather(jnp.concatenate([own_mean, own_second], axis=1), "col", axis=0)
    row_mean = jnp.mean(stats[:, :, 0], axis=0)[:, None]
    spread = (stats[:, :, 0] - row_mean[:, 0]) ** 2
    variance = (jnp.sum(stats[:, :, 1], axis=0) + width * jnp.sum(spread, axis=0))[:, None] / features
    inv_std = lax.rsqrt(variance + 1e-06)
    unit_rows = (values - row_mean) * inv_std
    gain_values = norm_gain.astype(jnp.float32)
    normed = chunk_of((unit_rows * gain_values).astype(jnp.bfloat16))
    hidden_part = jnp.dot(normed, inner_weight, preferred_element_type=jnp.float32)
    hidden_pre = lax.psum_scatter(
        hidden_part, "row", scatter_dimension=0, tiled=True
    )
    gelu_value, gelu_slope = gelu_parts(hidden_pre)
    activated = lax.all_gather(gelu_value.astype(jnp.bfloat16), "row", axis=0, tiled=True)
    act_part = contract_cols(cot_chunk, outer_weight)
    grad_act = lax.psum_scatter(
        act_part, "row", scatter_dimension=0, tiled=True
    )
    grad_pre = lax.all_gather(
        (grad_act * gelu_slope).astype(jnp.bfloat16), "row", axis=0, tiled=True
    )
    branch_out = share_of(
        jnp.dot(activated, outer_weight, preferred_element_type=jnp.float32)
    ).astype(jnp.bfloat16)
    grad_normed = share_of(contract_cols(grad_pre, inner_weight))
    grad_outer = contract_rows(activated, cot_chunk)
    grad_inner = contract_rows(normed, grad_pre)
    grad_gain = lax.psum(jnp.sum(grad_normed * unit_rows, axis=0), "row")
    grad_hat = grad_normed * gain_values
    sums = lax.psum(
        jnp.stack([jnp.sum(grad_hat, axis=1), jnp.sum(grad_hat * unit_rows, axis=1)]), "col"
    )
    first_mean = sums[0][:, None] / features
    second_mean = sums[1][:, None] / features
    grad_tokens = (inv_std * (grad_hat - first_mean - unit_rows * second_mean)).astype(
        jnp.bfloat16
    )
    return (branch_out, grad_tokens, grad_gain, grad_inner, grad_outer)


def solution(mesh):
    return jax.shard_map(
        body,
        mesh=mesh,
        in_specs=(P("row", "col"), P("col"), P("row", "col"), P("col", "row"), P("row", "col")),
        out_specs=(P("row", "col"), P("row", "col"), P("col"), P("row", "col"), P("col", "row")),
        check_vma=False,
    )
```

```python
import jax
import jax.numpy as jnp
from jax import lax
from jax.experimental import pallas as pl
from jax.experimental.pallas import tpu as pltpu
from jax.sharding import PartitionSpec as P

inv_sqrt_two = 0.7071067811865476
inv_sqrt_tau = 0.3989422804014327
MESH = pl.DeviceIdType.MESH
BF16 = jnp.bfloat16
F32 = jnp.float32

ROWS, SHARE = 384, 192
HALF, QUARTER = 192, 96
GROUP, CHUNK = 384, 1536
HID, PAIR = 384, 768
FEATURES = 6144
COPIES = 160


def gelu_parts(hidden_pre):
    cumulative = 0.5 * (1.0 + lax.erf(hidden_pre * inv_sqrt_two))
    density = jnp.exp(-0.5 * hidden_pre * hidden_pre) * inv_sqrt_tau
    return (hidden_pre * cumulative, cumulative + hidden_pre * density)


def dot_nn(left, right):
    return jnp.dot(left, right, preferred_element_type=F32)


def dot_nt(left, right):
    return lax.dot_general(
        left, right, (((1,), (1,)), ((), ())), preferred_element_type=F32
    )


def dot_tn(left, right):
    return lax.dot_general(
        left, right, (((0,), (0,)), ((), ())), preferred_element_type=F32
    )


def turn(index, by):
    return lax.rem(index + (by % 4), 4)


def to_rows(first, second):
    lane = lax.broadcasted_iota(jnp.int32, (ROWS, 128), 1)
    both = jnp.where(lane == 0, first, jnp.where(lane == 1, second, 0.0))
    return both.T[:8]


def to_columns(rows):
    full = jnp.concatenate([rows, jnp.zeros((120, ROWS), F32)], axis=0).T
    return full[:, 0:1], full[:, 1:2]


def merge_moments(parts, count):
    mean = sum(p[0:1] for p in parts) * (1.0 / len(parts))
    second = sum(p[1:2] + count * (p[0:1] - mean) ** 2 for p in parts)
    return jnp.concatenate([mean, second, jnp.zeros((6, ROWS), F32)], axis=0)


def kernel(
    tok_ref, gain_ref, w_in, w_out, cot_ref,
    branch_ref, gtok_ref, ggain_ref, ginner_ref, gouter_ref,
    w1, w2, unit, stat, tail, ggbuf,
    give_tok, mrg_tok, mrg_cot, own_tok, own_cot, g_tok, g_cot, n_tok, n_cot,
    hf, hb_tok, hb_cot, y1_tok, y1_cot, y2_tok, y2_cot, h_tok, h_cot,
    act, gpre,
    pb_out, pb_gn, r1_out, r1_gn, r2_out, r2_gn, s_out, s_gn, r3_out, r3_gn, r4_out, r4_gn,
    f_out, f_gn, o_out, o_gn, c_out, c_gn, d_out, d_gn,
    go_own, go_send, go_recv, gi_own, gi_send, gi_recv,
    send_sem, recv_sem, local_sem,
):
    y = lax.axis_index("row")
    col = lax.axis_index("col")
    z, x, q = col // 8, lax.rem(col // 2, 4), lax.rem(col, 2)
    p = 1 - q
    a0, b0 = p * x + q * z, p * z + q * x
    am, ap, a2 = turn(a0, -1), turn(a0, 1), turn(a0, 2)
    bm, bp, b2 = turn(b0, -1), turn(b0, 1), turn(b0, 2)
    ym, yp, y2 = turn(y, -1), turn(y, 1), turn(y, 2)
    first, second = q == 0, y != z

    def device(yy, zz, xx, qq):
        return (yy, zz * 8 + xx * 2 + qq)

    def on_a(by):
        return device(y, lax.rem(z + q * (by % 4), 4), lax.rem(x + p * (by % 4), 4), q)

    def on_b(by):
        return device(y, lax.rem(z + p * (by % 4), 4), lax.rem(x + q * (by % 4), 4), q)

    def on_y(by):
        return device(turn(y, by), z, x, q)

    mate = device(y, z, x, p)
    mirror = device(z, y, x, q)
    started, count = [], [0]

    def copy(src, dst, to):
        at = count[0]
        count[0] += 1
        return pltpu.make_async_remote_copy(
            src_ref=src, dst_ref=dst, send_sem=send_sem.at[at], recv_sem=recv_sem.at[at],
            device_id=to, device_id_type=MESH,
        )

    def send(src, dst, to):
        c = copy(src, dst, to)
        c.start()
        started.append(c)
        return c

    def rows_of(half):
        return pl.ds(pl.multiple_of(half * HALF, HALF), HALF)

    top, bottom = pl.ds(0, QUARTER), pl.ds(QUARTER, QUARTER)

    barrier = pltpu.get_barrier_semaphore()
    others = [mate] + [on(by) for on in (on_a, on_b, on_y) for by in (1, 2, 3)]
    for other in others:
        pl.semaphore_signal(barrier, inc=1, device_id=other, device_id_type=MESH)

    @pl.when(second)
    def _():
        pl.semaphore_signal(barrier, inc=1, device_id=mirror, device_id_type=MESH)
        pl.semaphore_wait(barrier, len(others) + 1)

    @pl.when(jnp.logical_not(second))
    def _():
        pl.semaphore_wait(barrier, len(others))

    give, keep = rows_of(p), rows_of(q)
    c_mrg_cot = send(cot_ref.at[give], mrg_cot, mate)
    hid_own = pl.ds(pl.multiple_of(q * HID, HID), HID)
    local_in = pltpu.make_async_copy(w_in, w1.at[:, hid_own], local_sem.at[0])
    local_out = pltpu.make_async_copy(w_out, w2.at[hid_own], local_sem.at[1])
    local_out.start()
    local_in.start()
    c_w2 = send(w_out, w2.at[hid_own], mate)
    c_w1 = send(w_in, w1.at[:, hid_own], mate)

    values = tok_ref[...].astype(F32)
    own_mean = jnp.sum(values, axis=1, keepdims=True) * (1.0 / SHARE)
    own_second = jnp.sum((values - own_mean) ** 2, axis=1, keepdims=True)
    stat[0] = to_rows(own_mean, own_second)
    c_stat = [send(stat.at[0], stat.at[1], mate)]

    def joined(a_half, b_half):
        return jnp.where(
            first,
            jnp.concatenate([a_half, b_half], axis=1),
            jnp.concatenate([b_half, a_half], axis=1),
        )

    def mirrored(piece, landing, at_home):
        c = copy(piece, landing, mirror)

        @pl.when(second)
        def _():
            c.start()

        @pl.when(jnp.logical_not(second))
        def _():
            at_home[...] = piece[...]

        return c

    def mirrored_wait(c):
        @pl.when(second)
        def _():
            c.wait_recv()

    def mirrored_sent(c):
        @pl.when(second)
        def _():
            c.wait_send()

    b_there, a_there = p * y + q * x, p * x + q * y

    c_mrg_cot.wait_recv()
    own_cot[...] = joined(
        cot_ref[keep].astype(F32), mrg_cot[...].astype(F32)
    ).astype(BF16)
    m_cot = mirrored(own_cot, g_cot.at[b_there, a_there], g_cot.at[b0, a0])

    c_stat[0].wait_recv()
    stat[2] = merge_moments([stat[0], stat[1]], SHARE)
    c_stat = [send(stat.at[2], stat.at[2 + by], on_a(by)) for by in (1, 2, 3)]
    for c in c_stat:
        c.wait_recv()
    stat[6] = merge_moments([stat[2 + by] for by in range(4)], 2 * SHARE)
    c_stat = [send(stat.at[6], stat.at[6 + by], on_b(by)) for by in (1, 2, 3)]
    for c in c_stat:
        c.wait_recv()
    stat[10] = merge_moments([stat[6 + by] for by in range(4)], 8 * SHARE)
    row_mean, total_second = to_columns(stat[10])
    inv_std = lax.rsqrt(total_second * (1.0 / FEATURES) + 1e-06)
    unit[...] = (tok_ref[...].astype(F32) - row_mean) * inv_std
    gain_values = gain_ref[...].astype(F32)
    normed_give = (unit[give] * gain_values).astype(BF16)
    give_tok[...] = normed_give
    c_mrg_tok = send(give_tok, mrg_tok, mate)

    class Gather:
        def __init__(self, g):
            self.g = g

        def own(self):
            g, home = self.g, self.g.at[b0, a0]
            self.ap, self.am = send(home, home, on_a(1)), send(home, home, on_a(-1))
            self.b = [(send(home, home, on_b(1)), send(home, home, on_b(-1)))]

        def near(self):
            g = self.g
            self.ap.wait_recv()
            left = g.at[b0, am]
            self.fa_top = send(left.at[top], left.at[top], on_a(1))
            self.b.append((send(left, left, on_b(1)), send(left, left, on_b(-1))))
            self.am.wait_recv()
            right = g.at[b0, ap]
            self.fa_bottom = send(right.at[bottom], right.at[bottom], on_a(-1))
            self.b.append((send(right, right, on_b(1)), send(right, right, on_b(-1))))
            self.fb = []

        def onward(self, i):
            g, a = self.g, (a0, am, ap, a2)[i]
            self.b[i][0].wait_recv()
            left = g.at[bm, a, top]
            up = send(left, left, on_b(1))
            self.b[i][1].wait_recv()
            right = g.at[bp, a, bottom]
            down = send(right, right, on_b(-1))
            self.fb.append((up, down))

        def far(self):
            self.fa_top.wait_recv()
            self.fa_bottom.wait_recv()
            last = self.g.at[b0, a2]
            self.b.append((send(last, last, on_b(1)), send(last, last, on_b(-1))))

        def end(self):
            for up, down in self.fb:
                up.wait_recv()
                down.wait_recv()

    def lay_out(g, n):
        def step(j, _):
            for s in range(4):
                piece = g[p * j + q * s, p * s + q * j]
                n[rows_of(j), s * GROUP : (s + 1) * GROUP] = piece
            return 0

        lax.fori_loop(0, 4, step, 0)

    cot_gather, tok_gather = Gather(g_cot), Gather(g_tok)
    mirrored_wait(m_cot)
    cot_gather.own()

    c_mrg_tok.wait_recv()
    own_tok[...] = joined(unit[keep] * gain_values, mrg_tok[...].astype(F32)).astype(BF16)
    m_tok = mirrored(own_tok, g_tok.at[b_there, a_there], g_tok.at[b0, a0])

    cot_gather.near()
    cot_gather.onward(0)
    cot_gather.far()
    cot_gather.onward(1)
    mirrored_wait(m_tok)
    tok_gather.own()
    cot_gather.onward(2)
    cot_gather.onward(3)
    tok_gather.near()
    tok_gather.onward(0)
    cot_gather.end()
    tok_gather.far()

    lay_out(g_cot, n_cot)
    local_out.wait()
    c_w2.wait_recv()

    class RowSum:
        def __init__(self, hb, r1, r2):
            self.hb, self.r1, self.r2 = hb, r1, r2

        def compute(self, product):
            def step(t, _):
                j = lax.rem(y + 2 + t, 4)
                value = product(j)
                hf[j] = value
                self.hb[j] = value.astype(BF16)
                return 0

            lax.fori_loop(0, 4, step, 0)
            hb, r1, r2 = self.hb, self.r1, self.r2
            self.up1 = send(hb.at[y2, top], r1.at[0], on_y(1))
            self.down1 = send(hb.at[y2, bottom], r1.at[1], on_y(-1))
            self.up2 = send(hb.at[yp, bottom], r2.at[0, bottom], on_y(1))
            self.down2 = send(hb.at[ym, top], r2.at[1, top], on_y(-1))

        def onward(self):
            hb, r1, r2 = self.hb, self.r1, self.r2
            self.up1.wait_recv()
            hb[yp, top] = (hf[yp, top] + r1[0].astype(F32)).astype(BF16)
            self.up3 = send(hb.at[yp, top], r2.at[0, top], on_y(1))
            self.down1.wait_recv()
            hb[ym, bottom] = (hf[ym, bottom] + r1[1].astype(F32)).astype(BF16)
            self.down3 = send(hb.at[ym, bottom], r2.at[1, bottom], on_y(-1))

        def end(self, out):
            out[...] = hf[y]

        def finish(self, out):
            for c in (self.up2, self.up3, self.down2, self.down3):
                c.wait_recv()
            out[...] += self.r2[0].astype(F32) + self.r2[1].astype(F32)

    cot_sum = RowSum(hb_cot, y1_cot, y2_cot)
    tok_sum = RowSum(hb_tok, y1_tok, y2_tok)
    cot_sum.compute(lambda j: dot_nt(n_cot[rows_of(j)], w2[...]))
    tok_gather.onward(1)
    tok_gather.onward(2)
    cot_sum.onward()
    cot_sum.end(h_cot)
    tok_gather.onward(3)
    tok_gather.end()
    lay_out(g_tok, n_tok)
    local_in.wait()
    c_w1.wait_recv()
    tok_sum.compute(lambda j: dot_nn(n_tok[rows_of(j)], w1[...]))
    cot_sum.finish(h_cot)
    tok_sum.onward()
    tok_sum.end(h_tok)
    tok_sum.finish(h_tok)

    gelu_value, gelu_slope = gelu_parts(h_tok[...])
    act[y] = gelu_value.astype(BF16)
    gpre[y] = (h_cot[...] * gelu_slope).astype(BF16)

    class RowGather:
        def __init__(self, g):
            self.g = g
            self.up, self.down = send(g.at[y], g.at[y], on_y(1)), send(g.at[y], g.at[y], on_y(-1))

        def onward(self):
            g = self.g
            self.up.wait_recv()
            self.fup = send(g.at[ym, top], g.at[ym, top], on_y(1))
            self.down.wait_recv()
            self.fdown = send(g.at[yp, bottom], g.at[yp, bottom], on_y(-1))

        def end(self):
            self.fup.wait_recv()
            self.fdown.wait_recv()

    act_gather = RowGather(act)
    gpre_gather = RowGather(gpre)
    act_gather.onward()
    act_gather.end()
    gpre_gather.onward()

    class PlaneSum:
        def __init__(self, pb, r1, r2, s, r3, r4, f):
            self.pb, self.r1, self.r2, self.s = pb, r1, r2, s
            self.r3, self.r4, self.f = r3, r4, f

        def compute(self, product):
            pb, r1, r2 = self.pb, self.r1, self.r2

            def step(j, _):
                value = product(j).astype(BF16)
                for s in range(4):
                    pb[p * j + q * s, p * s + q * j] = value[:, s * GROUP : (s + 1) * GROUP]
                return 0

            lax.fori_loop(0, 4, step, 0)
            self.up1 = send(pb.at[b2, :, top], r1.at[0], on_b(1))
            self.down1 = send(pb.at[b2, :, bottom], r1.at[1], on_b(-1))
            self.up2 = send(pb.at[bp, :, bottom], r2.at[0, :, bottom], on_b(1))
            self.down2 = send(pb.at[bm, :, top], r2.at[1, :, top], on_b(-1))

        def onward(self):
            pb, r1, r2 = self.pb, self.r1, self.r2
            self.up1.wait_recv()
            pb[bp, :, top] = (pb[bp, :, top].astype(F32) + r1[0].astype(F32)).astype(BF16)
            self.up3 = send(pb.at[bp, :, top], r2.at[0, :, top], on_b(1))
            self.down1.wait_recv()
            pb[bm, :, bottom] = (pb[bm, :, bottom].astype(F32) + r1[1].astype(F32)).astype(BF16)
            self.down3 = send(pb.at[bm, :, bottom], r2.at[1, :, bottom], on_b(-1))

        def cross(self):
            pb, r2, s, r3, r4 = self.pb, self.r2, self.s, self.r3, self.r4
            for c in (self.up2, self.down2, self.up3, self.down3):
                c.wait_recv()

            def summed(a):
                return pb[b0, a].astype(F32) + r2[0, a].astype(F32) + r2[1, a].astype(F32)

            s[a2] = summed(a2).astype(BF16)
            self.up4 = send(s.at[a2, top], r3.at[0], on_a(1))
            self.down4 = send(s.at[a2, bottom], r3.at[1], on_a(-1))
            s[ap] = summed(ap).astype(BF16)
            self.up5 = send(s.at[ap, bottom], r4.at[0, bottom], on_a(1))
            s[am] = summed(am).astype(BF16)
            self.down5 = send(s.at[am, top], r4.at[1, top], on_a(-1))
            self.f[...] = summed(a0)

        def near(self):
            s, r3, r4 = self.s, self.r3, self.r4
            self.up4.wait_recv()
            s[ap, top] = (s[ap, top].astype(F32) + r3[0].astype(F32)).astype(BF16)
            self.up6 = send(s.at[ap, top], r4.at[0, top], on_a(1))
            self.down4.wait_recv()
            s[am, bottom] = (s[am, bottom].astype(F32) + r3[1].astype(F32)).astype(BF16)
            self.down6 = send(s.at[am, bottom], r4.at[1, bottom], on_a(-1))

        def end(self):
            for c in (self.up5, self.down5, self.up6, self.down6):
                c.wait_recv()
            return self.f[...] + self.r4[0].astype(F32) + self.r4[1].astype(F32)

    out_sum = PlaneSum(pb_out, r1_out, r2_out, s_out, r3_out, r4_out, f_out)
    gn_sum = PlaneSum(pb_gn, r1_gn, r2_gn, s_gn, r3_gn, r4_gn, f_gn)
    out_sum.compute(lambda j: dot_nn(act[j], w2[...]))
    gpre_gather.end()
    gn_sum.compute(lambda j: dot_nt(gpre[j], w1[...]))
    out_sum.onward()

    def by_hidden(t, who):
        return pl.ds(pl.multiple_of(who * HID, HID), HID)

    def grad_outer(who, into):
        left = act[:, :, by_hidden(0, who)].reshape(4 * HALF, HID)
        into[...] = dot_tn(left, n_cot[...])

    def grad_inner(who, into):
        right = gpre[:, :, by_hidden(0, who)].reshape(4 * HALF, HID)

        def step(t, _):
            at = pl.ds(pl.multiple_of(t * GROUP, GROUP), GROUP)
            into[at] = dot_tn(n_tok[:, at], right)
            return 0

        lax.fori_loop(0, 4, step, 0)

    grad_outer(p, go_send)
    c_go = send(go_send, go_recv, mate)
    out_sum.cross()
    gn_sum.onward()
    grad_inner(p, gi_send)
    c_gi = send(gi_send, gi_recv, mate)
    out_sum.near()
    out_total = out_sum.end()
    f_piece_out = s_out.at[a0]
    s_out[a0] = out_total.astype(BF16)
    m_out = mirrored(f_piece_out, o_out, o_out)
    gn_sum.cross()
    grad_outer(q, go_own)
    gn_sum.near()
    gn_total = gn_sum.end()
    s_gn[a0] = gn_total.astype(BF16)
    m_gn = mirrored(s_gn.at[a0], o_gn, o_gn)
    grad_inner(q, gi_own)

    def split(o, to_mate, landing):
        piece = o[...].astype(F32)
        left, right = piece[:, 0:SHARE], piece[:, SHARE:GROUP]
        own = jnp.where(first, left, right)
        to_mate[...] = jnp.where(first, right, left).astype(BF16)
        return own, send(to_mate, landing, mate)

    mirrored_wait(m_out)
    own, c_out_mate = split(o_out, c_out, d_out)
    branch_ref[keep] = own.astype(BF16)

    mirrored_wait(m_gn)
    own_gn, c_gn_mate = split(o_gn, c_gn, d_gn)
    c_go.wait_recv()
    go_own[...] += go_recv[...]
    out_go = pltpu.make_async_copy(go_own, gouter_ref, local_sem.at[2])
    out_go.start()
    c_gi.wait_recv()
    gi_own[...] += gi_recv[...]
    out_gi = pltpu.make_async_copy(gi_own, ginner_ref, local_sem.at[3])
    out_gi.start()

    c_out_mate.wait_recv()
    branch_ref[give] = d_out[...]
    c_gn_mate.wait_recv()
    unit_rows = unit[...]
    tail[0, keep] = own_gn
    tail[0, give] = d_gn[...].astype(F32)
    grad_normed = tail[0]
    grad_hat = grad_normed * gain_values
    weighted = grad_hat * unit_rows
    ggbuf[0] = jnp.broadcast_to(
        jnp.sum(grad_normed * unit_rows, axis=0, keepdims=True), (8, SHARE)
    )
    c_gg = [send(ggbuf.at[0], ggbuf.at[by], on_y(by)) for by in (1, 2, 3)]
    stat[11] = to_rows(
        jnp.sum(grad_hat, axis=1, keepdims=True), jnp.sum(weighted, axis=1, keepdims=True)
    )
    c_stat = [send(stat.at[11], stat.at[12], mate)]
    c_stat[0].wait_recv()
    stat[13] = stat[11] + stat[12]
    c_stat = [send(stat.at[13], stat.at[13 + by], on_a(by)) for by in (1, 2, 3)]
    for c in c_stat:
        c.wait_recv()
    stat[17] = stat[13] + stat[14] + stat[15] + stat[16]
    c_stat = [send(stat.at[17], stat.at[17 + by], on_b(by)) for by in (1, 2, 3)]
    for c in c_stat:
        c.wait_recv()
    sums = (stat[17] + stat[18] + stat[19] + stat[20]) * (1.0 / FEATURES)
    first_mean, second_mean = to_columns(sums)
    row_mean, total_second = to_columns(stat[10])
    inv_std = lax.rsqrt(total_second * (1.0 / FEATURES) + 1e-06)
    gtok_ref[...] = (inv_std * (grad_hat - first_mean - unit_rows * second_mean)).astype(BF16)
    for c in c_gg:
        c.wait_recv()
    ggain_ref[...] = (ggbuf[0] + ggbuf[1] + ggbuf[2] + ggbuf[3])[0:1]

    for c in started:
        c.wait_send()
    for c in (m_cot, m_tok, m_out, m_gn):
        mirrored_sent(c)
    out_go.wait()
    out_gi.wait()


def scratch():
    def buf(*shape, kind=BF16):
        return pltpu.VMEM(shape, kind)

    twice = lambda *shape, kind=BF16: [buf(*shape, kind=kind), buf(*shape, kind=kind)]
    return [
        buf(CHUNK, PAIR), buf(PAIR, CHUNK),
        buf(ROWS, SHARE, kind=F32), buf(21, 8, ROWS, kind=F32),
        buf(1, ROWS, SHARE, kind=F32), buf(4, 8, SHARE, kind=F32),
        buf(HALF, SHARE), *twice(HALF, SHARE), *twice(HALF, GROUP),
        *twice(4, 4, HALF, GROUP), *twice(4 * HALF, CHUNK),
        buf(4, HALF, PAIR, kind=F32), *twice(4, HALF, PAIR),
        *twice(2, QUARTER, PAIR), *twice(2, HALF, PAIR),
        *twice(HALF, PAIR, kind=F32),
        *twice(4, HALF, PAIR),
        *twice(4, 4, HALF, GROUP),
        *twice(2, 4, QUARTER, GROUP), *twice(2, 4, HALF, GROUP),
        *twice(4, HALF, GROUP), *twice(2, QUARTER, GROUP),
        *twice(2, HALF, GROUP), *twice(HALF, GROUP, kind=F32),
        *twice(HALF, GROUP), *twice(HALF, SHARE), *twice(HALF, SHARE),
        buf(HID, CHUNK, kind=F32), buf(HID, CHUNK, kind=F32), buf(HID, CHUNK, kind=F32),
        buf(CHUNK, HID, kind=F32), buf(CHUNK, HID, kind=F32), buf(CHUNK, HID, kind=F32),
        pltpu.SemaphoreType.DMA((COPIES,)),
        pltpu.SemaphoreType.DMA((COPIES,)),
        pltpu.SemaphoreType.DMA((4,)),
    ]


def body(tokens, norm_gain, inner_weight, outer_weight, cotangent):
    vmem, anywhere = pl.BlockSpec(memory_space=pltpu.VMEM), pl.BlockSpec(memory_space=pl.ANY)
    outs = pl.pallas_call(
        kernel,
        out_shape=[
            jax.ShapeDtypeStruct((ROWS, SHARE), BF16),
            jax.ShapeDtypeStruct((ROWS, SHARE), BF16),
            jax.ShapeDtypeStruct((1, SHARE), F32),
            jax.ShapeDtypeStruct((CHUNK, HID), F32),
            jax.ShapeDtypeStruct((HID, CHUNK), F32),
        ],
        in_specs=[vmem, vmem, anywhere, anywhere, vmem],
        out_specs=[vmem, vmem, vmem, anywhere, anywhere],
        scratch_shapes=scratch(),
        compiler_params=pltpu.CompilerParams(
            collective_id=0, has_side_effects=True, vmem_limit_bytes=60 * 1024 * 1024
        ),
        name="mlp_block",
    )(tokens, norm_gain.reshape(1, SHARE), inner_weight, outer_weight, cotangent)
    branch_out, grad_tokens, grad_gain, grad_inner, grad_outer = outs
    return (branch_out, grad_tokens, grad_gain.reshape(SHARE), grad_inner, grad_outer)


def solution(mesh):
    return jax.shard_map(
        body,
        mesh=mesh,
        in_specs=(P("row", "col"), P("col"), P("row", "col"), P("col", "row"), P("row", "col")),
        out_specs=(P("row", "col"), P("row", "col"), P("col"), P("row", "col"), P("col", "row")),
        check_vma=False,
    )
```

```python
import functools

import jax
import jax.numpy as jnp
from jax import lax
from jax.experimental import pallas as pl
from jax.experimental.pallas import tpu as pltpu
from jax.sharding import PartitionSpec as P

inv_sqrt_two = 0.7071067811865476
inv_sqrt_tau = 0.3989422804014327
MESH = pl.DeviceIdType.MESH
BF16 = jnp.bfloat16
F32 = jnp.float32

ROWS, SHARE = 384, 192
HALF, PART = 192, 96
GROUP, CHUNK = 384, 1536
HID, PAIR = 384, 768
FEATURES = 6144
COPIES = 260
VMEM_BYTES = 54 * 1024 * 1024
ORDER = (
    "start", "mC", "s1", "g1", "s2", "C0.own", "C1.own", "g2", "s3", "C0.near", "C0.on0",
    "mT", "C1.near", "C1.on0", "C0.far", "g3", "C0.on1", "C0.on2", "C1.far", "C1.on1",
    "C1.on2", "T0.own", "C0.on3", "T1.own", "C1.on3", "T0.near", "T0.on0", "C0.end",
    "C0.cmp", "T1.on0", "T0.far", "T0.on1", "T1.near", "T0.on2", "C1.end", "C1.cmp",
    "T0.on3", "C0.rson", "T1.far", "T1.on1", "T1.on2", "T0.end", "T0.cmp", "T1.on3",
    "C1.rson", "T1.end", "T0.rson", "T1.cmp", "act0", "gpre0", "T1.rson", "act0.on",
    "gpre0.on", "act1", "gpre1", "ms", "out0.cmp", "gn0.cmp", "mt", "act1.on", "out0.on",
    "gpre1.on", "gn0.on", "mu", "gn1.cmp", "out0.cross", "gn0.cross", "GIs", "gn1.on",
    "out1.cmp", "GOo", "out0.near", "gn1.cross", "out1.on", "gn0.near", "GOs", "gn1.near",
    "out0.end", "out1.cross", "gn0.end", "gn1.end", "out1.near", "GIo", "out1.end", "GOx",
    "spG", "fin0", "spO", "GIx", "outx", "fin1",
)
FIRST_COT, FIRST_PART = "C0", 0


def gelu_parts(hidden_pre):
    cumulative = 0.5 * (1.0 + lax.erf(hidden_pre * inv_sqrt_two))
    density = jnp.exp(-0.5 * hidden_pre * hidden_pre) * inv_sqrt_tau
    return (hidden_pre * cumulative, cumulative + hidden_pre * density)


def dot_nn(left, right):
    return jnp.dot(left, right, preferred_element_type=F32)


def dot_nt(left, right):
    return lax.dot_general(
        left, right, (((1,), (1,)), ((), ())), preferred_element_type=F32
    )


def dot_tn(left, right):
    return lax.dot_general(
        left, right, (((0,), (0,)), ((), ())), preferred_element_type=F32
    )


def turn(index, by):
    return lax.rem(index + (by % 4), 4)


def merge_moments(parts, count):
    mean = sum(p[0:1] for p in parts) * (1.0 / len(parts))
    second = sum(p[1:2] + count * (p[0:1] - mean) ** 2 for p in parts)
    return jnp.concatenate([mean, second, jnp.zeros((6, ROWS), F32)], axis=0)


def kernel(
    tok_ref, gain_ref, w_in, w_out, cot_ref,
    branch_ref, gtok_ref, ggain_ref, ginner_ref, gouter_ref,
    w1, w2, unit, stat, ggbuf, gz, gx, gy, hidden, slope, sums, ms, nat_tok, nat_cot,
    mrg_tok, mrg_cot, own_tok, own_cot, g_tok, g_cot, n_tok, n_cot,
    hf_tok, hf_cot, hb_tok, hb_cot, y1_tok, y1_cot, y2_tok, y2_cot,
    act, gpre,
    pb_out, pb_gn, r1_out, r1_gn, r2_out, r2_gn, s_out, s_gn, r3_out, r3_gn, r4_out, r4_gn,
    f_out, f_gn, o_out, o_gn, c_out, c_gn, d_out, d_gn,
    go_own, go_send, go_recv, gi_own, gi_send, gi_recv,
    send_sem, recv_sem, local_sem,
):
    y = lax.axis_index("row")
    col = lax.axis_index("col")
    z, x, q = col // 8, lax.rem(col // 2, 4), lax.rem(col, 2)
    p = 1 - q
    a0, b0 = p * x + q * z, p * z + q * x
    am, ap, a2 = turn(a0, -1), turn(a0, 1), turn(a0, 2)
    bm, bp, b2 = turn(b0, -1), turn(b0, 1), turn(b0, 2)
    ym, yp, y2 = turn(y, -1), turn(y, 1), turn(y, 2)
    first, second = q == 0, y != z

    def device(yy, zz, xx, qq):
        return (yy, zz * 8 + xx * 2 + qq)

    def on_a(by):
        return device(y, lax.rem(z + q * (by % 4), 4), lax.rem(x + p * (by % 4), 4), q)

    def on_b(by):
        return device(y, lax.rem(z + p * (by % 4), 4), lax.rem(x + q * (by % 4), 4), q)

    def on_y(by):
        return device(turn(y, by), z, x, q)

    mate = device(y, z, x, p)
    mirror = device(z, y, x, q)
    started, count = [], [0]

    def copy(src, dst, to):
        at = count[0]
        count[0] += 1
        return pltpu.make_async_remote_copy(
            src_ref=src, dst_ref=dst, send_sem=send_sem.at[at], recv_sem=recv_sem.at[at],
            device_id=to, device_id_type=MESH,
        )

    def send(src, dst, to):
        c = copy(src, dst, to)
        c.start()
        started.append(c)
        return c

    def left(c):
        c.wait_send()
        started[:] = [other for other in started if other is not c]

    def rows_of(half):
        return pl.ds(pl.multiple_of(half * HALF, HALF), HALF)

    top, bottom = pl.ds(0, PART // 2), pl.ds(PART // 2, PART // 2)

    barrier = pltpu.get_barrier_semaphore()
    others = [mate] + [on(by) for on in (on_a, on_b, on_y) for by in (1, 2, 3)]
    for other in others:
        pl.semaphore_signal(barrier, inc=1, device_id=other, device_id_type=MESH)

    @pl.when(second)
    def _():
        pl.semaphore_signal(barrier, inc=1, device_id=mirror, device_id_type=MESH)

    hid_own = pl.ds(pl.multiple_of(q * HID, HID), HID)
    local_in = pltpu.make_async_copy(w_in, w1.at[:, hid_own], local_sem.at[0])
    local_out = pltpu.make_async_copy(w_out, w2.at[hid_own], local_sem.at[1])
    local_out.start()
    local_in.start()
    nat_cot[...] = cot_ref[...].astype(F32).T.astype(BF16)

    values = tok_ref[...].astype(F32)
    own_mean = jnp.sum(values, axis=0, keepdims=True) * (1.0 / SHARE)
    own_second = jnp.sum((values - own_mean) ** 2, axis=0, keepdims=True)
    stat[0] = jnp.concatenate([own_mean, own_second, jnp.zeros((6, ROWS), F32)], axis=0)
    gz[z] = jnp.broadcast_to(gain_ref[...].astype(F32).reshape(1, SHARE), (8, SHARE))

    @pl.when(second)
    def _():
        pl.semaphore_wait(barrier, len(others) + 1)

    @pl.when(jnp.logical_not(second))
    def _():
        pl.semaphore_wait(barrier, len(others))

    def joined(own, other):
        return jnp.where(
            first,
            jnp.concatenate([own, other], axis=1),
            jnp.concatenate([other, own], axis=1),
        )

    def mirrored(piece, landing, at_home):
        c = copy(piece, landing, mirror)

        @pl.when(second)
        def _():
            c.start()

        @pl.when(jnp.logical_not(second))
        def _():
            at_home[...] = piece[...]

        return c

    def mirrored_wait(c):
        @pl.when(second)
        def _():
            c.wait_recv()

    def mirrored_sent(c):
        @pl.when(second)
        def _():
            c.wait_send()

    b_there, a_there = p * y + q * x, p * x + q * y

    class Gather:
        def __init__(self, g, part):
            self.g, self.part = g, part

        def at(self, b, a, side=None):
            rows = {None: (0, PART), 0: (0, PART // 2), 1: (PART // 2, PART // 2)}[side]
            return self.g.at[b, a, pl.ds(self.part * PART + rows[0], rows[1])]

        def own(self):
            home = self.at(b0, a0)
            self.fb = []
            self.ap, self.am = send(home, home, on_a(1)), send(home, home, on_a(-1))
            self.b = [(send(home, home, on_b(1)), send(home, home, on_b(-1)))]

        def near(self):
            self.ap.wait_recv()
            left, some = self.at(b0, am), self.at(b0, am, 0)
            self.fa_top = send(some, some, on_a(1))
            self.b.append((send(left, left, on_b(1)), send(left, left, on_b(-1))))
            self.am.wait_recv()
            right, some = self.at(b0, ap), self.at(b0, ap, 1)
            self.fa_bottom = send(some, some, on_a(-1))
            self.b.append((send(right, right, on_b(1)), send(right, right, on_b(-1))))

        def onward(self, i):
            a = (a0, am, ap, a2)[i]
            self.b[i][0].wait_recv()
            left = self.at(bm, a, 0)
            up = send(left, left, on_b(1))
            self.b[i][1].wait_recv()
            right = self.at(bp, a, 1)
            down = send(right, right, on_b(-1))
            self.fb.append((up, down))

        def far(self):
            self.fa_top.wait_recv()
            self.fa_bottom.wait_recv()
            last = self.at(b0, a2)
            self.b.append((send(last, last, on_b(1)), send(last, last, on_b(-1))))

        def end(self, n):
            for up, down in self.fb:
                up.wait_recv()
                down.wait_recv()
            rows = pl.ds(self.part * PART, PART)
            for j in range(4):
                for s in range(4):
                    to = pl.ds((self.part * 4 + j) * PART, PART)
                    n[to, s * GROUP : (s + 1) * GROUP] = self.g[p * j + q * s, p * s + q * j, rows]

    class RowSum:
        def __init__(self, hf, hb, r1, r2, part):
            self.hf, self.hb = hf.at[part], hb.at[part]
            self.r1, self.r2 = r1.at[part], r2.at[part]

        def compute(self, value):
            hf, hb, r1, r2 = self.hf, self.hb, self.r1, self.r2
            for j in range(4):
                block = value[j * PART : (j + 1) * PART]
                hf[j] = block
                hb[j] = block.astype(BF16)
            self.up1 = send(hb.at[y2, top], r1.at[0], on_y(1))
            self.down1 = send(hb.at[y2, bottom], r1.at[1], on_y(-1))
            self.up2 = send(hb.at[yp, bottom], r2.at[0, bottom], on_y(1))
            self.down2 = send(hb.at[ym, top], r2.at[1, top], on_y(-1))

        def onward(self):
            hf, hb, r1, r2 = self.hf, self.hb, self.r1, self.r2
            self.up1.wait_recv()
            hb[yp, top] = (hf[yp, top] + r1[0].astype(F32)).astype(BF16)
            self.up3 = send(hb.at[yp, top], r2.at[0, top], on_y(1))
            self.down1.wait_recv()
            hb[ym, bottom] = (hf[ym, bottom] + r1[1].astype(F32)).astype(BF16)
            self.down3 = send(hb.at[ym, bottom], r2.at[1, bottom], on_y(-1))

        def end(self):
            for c in (self.up2, self.up3, self.down2, self.down3):
                c.wait_recv()
            return self.hf[y] + self.r2[0].astype(F32) + self.r2[1].astype(F32)

    class RowGather:
        def __init__(self, g, part, block):
            g = self.g = g.at[part]
            g[y] = block
            self.up, self.down = send(g.at[y], g.at[y], on_y(1)), send(g.at[y], g.at[y], on_y(-1))

        def onward(self):
            g = self.g
            self.up.wait_recv()
            self.fup = send(g.at[ym, top], g.at[ym, top], on_y(1))
            self.down.wait_recv()
            self.fdown = send(g.at[yp, bottom], g.at[yp, bottom], on_y(-1))

        def end(self):
            self.fup.wait_recv()
            self.fdown.wait_recv()
            return self.g[...].reshape(4 * PART, PAIR)

    class PlaneSum:
        def __init__(self, pb, r1, r2, s, r3, r4, f, o, part):
            self.pb, self.r1, self.r2, self.s = pb.at[part], r1.at[part], r2.at[part], s.at[part]
            self.r3, self.r4, self.f = r3.at[part], r4.at[part], f.at[part]
            self.o = o.at[part]

        def compute(self, product):
            pb, r1, r2 = self.pb, self.r1, self.r2
            for wide in range(2):
                value = product(wide * 2 * GROUP, 2 * GROUP)
                for j in range(4):
                    for t in range(2):
                        s = wide * 2 + t
                        pb[p * j + q * s, p * s + q * j] = value[
                            j * PART : (j + 1) * PART, t * GROUP : (t + 1) * GROUP
                        ].astype(BF16)
            self.up1 = send(pb.at[b2, :, top], r1.at[0], on_b(1))
            self.down1 = send(pb.at[b2, :, bottom], r1.at[1], on_b(-1))
            self.up2 = send(pb.at[bp, :, bottom], r2.at[0, :, bottom], on_b(1))
            self.down2 = send(pb.at[bm, :, top], r2.at[1, :, top], on_b(-1))

        def onward(self):
            pb, r1, r2 = self.pb, self.r1, self.r2
            self.up1.wait_recv()
            pb[bp, :, top] = (pb[bp, :, top].astype(F32) + r1[0].astype(F32)).astype(BF16)
            self.up3 = send(pb.at[bp, :, top], r2.at[0, :, top], on_b(1))
            self.down1.wait_recv()
            pb[bm, :, bottom] = (pb[bm, :, bottom].astype(F32) + r1[1].astype(F32)).astype(BF16)
            self.down3 = send(pb.at[bm, :, bottom], r2.at[1, :, bottom], on_b(-1))

        def cross(self):
            pb, r2, s, r3, r4 = self.pb, self.r2, self.s, self.r3, self.r4
            for c in (self.up2, self.down2, self.up3, self.down3):
                c.wait_recv()

            def summed(a):
                return pb[b0, a].astype(F32) + r2[0, a].astype(F32) + r2[1, a].astype(F32)

            s[a2] = summed(a2).astype(BF16)
            self.up4 = send(s.at[a2, top], r3.at[0], on_a(1))
            self.down4 = send(s.at[a2, bottom], r3.at[1], on_a(-1))
            s[ap] = summed(ap).astype(BF16)
            self.up5 = send(s.at[ap, bottom], r4.at[0, bottom], on_a(1))
            s[am] = summed(am).astype(BF16)
            self.down5 = send(s.at[am, top], r4.at[1, top], on_a(-1))
            self.f[...] = summed(a0)

        def near(self):
            s, r3, r4 = self.s, self.r3, self.r4
            self.up4.wait_recv()
            s[ap, top] = (s[ap, top].astype(F32) + r3[0].astype(F32)).astype(BF16)
            self.up6 = send(s.at[ap, top], r4.at[0, top], on_a(1))
            self.down4.wait_recv()
            s[am, bottom] = (s[am, bottom].astype(F32) + r3[1].astype(F32)).astype(BF16)
            self.down6 = send(s.at[am, bottom], r4.at[1, bottom], on_a(-1))

        def end(self):
            for c in (self.up5, self.down5, self.up6, self.down6):
                c.wait_recv()
            total = self.f[...] + self.r4[0].astype(F32) + self.r4[1].astype(F32)
            self.s[a0] = total.astype(BF16)
            self.m = mirrored(self.s.at[a0], self.o, self.o)

    give, keep = rows_of(p), rows_of(q)
    gain_column = []
    gather = {f"C{m}": Gather(g_cot, m) for m in range(2)}
    gather |= {f"T{m}": Gather(g_tok, m) for m in range(2)}
    row_sum = {f"C{m}": RowSum(hf_cot, hb_cot, y1_cot, y2_cot, m) for m in range(2)}
    row_sum |= {f"T{m}": RowSum(hf_tok, hb_tok, y1_tok, y2_tok, m) for m in range(2)}
    row_gather, plane_sum, c = {}, {}, {}
    for m in range(2):
        plane_sum[f"out{m}"] = PlaneSum(
            pb_out, r1_out, r2_out, s_out, r3_out, r4_out, f_out, o_out, m
        )
        plane_sum[f"gn{m}"] = PlaneSum(pb_gn, r1_gn, r2_gn, s_gn, r3_gn, r4_gn, f_gn, o_gn, m)

    def three(src, buffer, first_slot, on):
        return [send(src, buffer.at[first_slot + by - 1], on(by)) for by in (1, 2, 3)]

    def arrived(copies):
        for one in copies:
            one.wait_recv()

    def on_z(by):
        return device(y, turn(z, by), x, q)

    def on_x(by):
        return device(y, z, turn(x, by), q)

    def start():
        c["mrg_cot"] = send(nat_cot.at[give], mrg_cot, mate)
        c["st0"] = send(stat.at[0], stat.at[1], mate)
        c["w2"] = send(w_out, w2.at[hid_own], mate)
        c["w1"] = send(w_in, w1.at[:, hid_own], mate)
        c["gz"] = [send(gz.at[z], gz.at[z], on_z(by)) for by in (1, 2, 3)]

    def cot_swap():
        c["mrg_cot"].wait_recv()
        own_cot[...] = joined(nat_cot[keep].astype(F32), mrg_cot[...].astype(F32)).astype(BF16)
        c["swC"] = mirrored(own_cot, g_cot.at[b_there, a_there], g_cot.at[b0, a0])

    def moments_cores():
        c["st0"].wait_recv()
        stat[2] = merge_moments([stat[0], stat[1]], SHARE)
        c["st1"] = three(stat.at[2], stat, 3, on_a)

    def moments_a():
        arrived(c["st1"])
        stat[6] = merge_moments([stat[2 + by] for by in range(4)], 2 * SHARE)
        c["st2"] = three(stat.at[6], stat, 7, on_b)

    def moments_b():
        arrived(c["st2"])
        moments = merge_moments([stat[6 + by] for by in range(4)], 8 * SHARE)
        inv_std = lax.rsqrt(moments[1:2] * (1.0 / FEATURES) + 1e-06)
        unit[...] = (tok_ref[...].astype(F32) - moments[0:1]) * inv_std
        stat[10] = jnp.broadcast_to(inv_std, (8, ROWS))
        gain_column.append(jnp.broadcast_to(gain_ref[...].astype(F32).reshape(1, SHARE), (128, SHARE)).T[:, 0:1])
        nat_tok[...] = (unit[...] * gain_column[0]).T.astype(BF16)
        c["mrg_tok"] = send(nat_tok.at[give], mrg_tok, mate)

    def tok_swap():
        c["mrg_tok"].wait_recv()
        own_tok[...] = joined(nat_tok[keep].astype(F32), mrg_tok[...].astype(F32)).astype(BF16)
        c["swT"] = mirrored(own_tok, g_tok.at[b_there, a_there], g_tok.at[b0, a0])

    def gain_z():
        arrived(c["gz"])
        c["gm"] = send(gz.at[y], gz.at[4], mate)

    def gain_cores():
        c["gm"].wait_recv()
        gx[x] = joined(gz[y], gz[4])
        c["gx"] = [send(gx.at[x], gx.at[x], on_x(by)) for by in (1, 2, 3)]

    def gain_x():
        arrived(c["gx"])
        local_in.wait()
        c["w1"].wait_recv()
        gy[0] = sum(
            dot_nn(gx[s].astype(BF16), w1[s * GROUP : (s + 1) * GROUP]) for s in range(4)
        )
        c["gy"] = three(gy.at[0], gy, 1, on_y)

    def part_rows(m):
        return pl.ds(m * 4 * PART, 4 * PART)

    def own_part(name):
        if name[1] == "0":
            mirrored_wait(c["sw" + name[0]])
        gather[name].own()

    def end_part(name):
        gather[name].end(n_cot if name[0] == "C" else n_tok)

    def compute(name):
        rows = part_rows(int(name[1]))
        if name[0] == "C":
            if name == FIRST_COT:
                local_out.wait()
                c["w2"].wait_recv()
            row_sum[name].compute(dot_nt(n_cot[rows], w2[...]))
        else:
            row_sum[name].compute(dot_nn(n_tok[rows], w1[...]))

    def gelu(m):
        hidden_pre = row_sum[f"T{m}"].end()
        gelu_value, slope[m] = gelu_parts(hidden_pre)
        hidden[m] = hidden_pre
        row_gather[f"act{m}"] = RowGather(act, m, gelu_value.astype(BF16))

    def gradient(m):
        if m == FIRST_PART:
            arrived(c["gy"])
        grad_pre = (row_sum[f"C{m}"].end() * slope[m]).astype(BF16)
        row_gather[f"gpre{m}"] = RowGather(gpre, m, grad_pre)
        grad_pre = grad_pre.astype(F32)
        gain_row = (gy[0] + gy[1] + gy[2] + gy[3])[0:1]
        one = jnp.sum(grad_pre * gain_row, axis=1, keepdims=True)
        two = jnp.sum(grad_pre * hidden[m], axis=1, keepdims=True)
        lane = lax.broadcasted_iota(jnp.int32, (PART, 128), 1)
        sums[m * PART : (m + 1) * PART] = jnp.where(lane == 0, one, two)

    def means_cores():
        ms[0] = sums[...].T[0:8]
        c["ms0"] = three(ms.at[0], ms, 1, on_a)

    def means_a():
        arrived(c["ms0"])
        ms[4] = ms[0] + ms[1] + ms[2] + ms[3]
        c["ms1"] = three(ms.at[4], ms, 5, on_b)

    def means_b():
        arrived(c["ms1"])
        ms[8] = (ms[4] + ms[5] + ms[6] + ms[7]) * (1.0 / FEATURES)
        c["ms2"] = send(ms.at[8], ms.at[9], mate)

    def out_compute(m):
        block = row_gather[f"act{m}"].end()
        plane_sum[f"out{m}"].compute(lambda at, wide: dot_nn(block, w2[:, at : at + wide]))

    def gn_compute(m):
        block = row_gather[f"gpre{m}"].end()
        plane_sum[f"gn{m}"].compute(lambda at, wide: dot_nt(block, w1[at : at + wide]))

    def by_hidden(who):
        return pl.ds(pl.multiple_of(who * HID, HID), HID)

    def grad_outer(who, into):
        block = act[:, :, :, by_hidden(who)].reshape(8 * PART, HID)
        into[...] = dot_tn(block, n_cot[...])

    def grad_inner(who, into):
        block = gpre[:, :, :, by_hidden(who)].reshape(8 * PART, HID)

        def step(t, _):
            at = pl.ds(pl.multiple_of(t * GROUP, GROUP), GROUP)
            into[at] = dot_tn(n_tok[:, at], block)
            return 0

        lax.fori_loop(0, 4, step, 0)

    def outer_send():
        grad_outer(p, go_send)
        c["go"] = send(go_send, go_recv, mate)

    def inner_send():
        grad_inner(p, gi_send)
        c["gi"] = send(gi_send, gi_recv, mate)

    def outer_add():
        c["go"].wait_recv()
        gouter_ref[...] = go_own[...] + go_recv[...]

    def inner_add():
        c["gi"].wait_recv()
        ginner_ref[...] = gi_own[...] + gi_recv[...]

    def split(name, o, to_mate, landing):
        for m in range(2):
            mirrored_wait(plane_sum[f"{name}{m}"].m)
        piece = o[...].reshape(HALF, GROUP).astype(F32)
        low, high = piece[:, 0:SHARE], piece[:, SHARE:GROUP]
        to_mate[...] = jnp.where(first, high, low).astype(BF16)
        return jnp.where(first, low, high).astype(BF16), send(to_mate, landing, mate)

    def out_split():
        left(c["mrg_cot"])
        nat_cot[keep], c["out"] = split("out", o_out, c_out, d_out)

    def gn_split():
        left(c["mrg_tok"])
        nat_tok[keep], c["gn"] = split("gn", o_gn, c_gn, d_gn)

    def out_end():
        c["out"].wait_recv()
        nat_cot[give] = d_out[...]
        branch_ref[...] = nat_cot[...].astype(F32).T.astype(BF16)

    def gn_end():
        c["gn"].wait_recv()
        nat_tok[give] = d_gn[...]
        unit_rows = unit[...]
        grad_normed = nat_tok[...].astype(F32).T
        gain_part = jnp.sum(grad_normed * unit_rows, axis=1, keepdims=True)
        ggbuf[0] = jnp.broadcast_to(gain_part, (SHARE, 128)).T[0:8]
        c["gg"] = three(ggbuf.at[0], ggbuf, 1, on_y)
        c["ms2"].wait_recv()
        means = joined(ms[8], ms[9])
        grad_hat = grad_normed * gain_column[0]
        gtok_ref[...] = (
            stat[10, 0:1] * (grad_hat - means[0:1] - unit_rows * means[1:2])
        ).astype(BF16)

    def gain_end():
        arrived(c["gg"])
        ggain_ref[...] = (ggbuf[0] + ggbuf[1] + ggbuf[2] + ggbuf[3])[0:1]

    events = {
        "start": start, "mC": cot_swap, "s1": moments_cores, "s2": moments_a, "s3": moments_b,
        "mT": tok_swap, "g1": gain_z, "g2": gain_cores, "g3": gain_x,
        "ms": means_cores, "mt": means_a, "mu": means_b,
        "GOs": outer_send, "GOo": lambda: grad_outer(q, go_own), "GOx": outer_add,
        "GIs": inner_send, "GIo": lambda: grad_inner(q, gi_own), "GIx": inner_add,
        "spO": out_split, "spG": gn_split, "outx": out_end, "fin0": gn_end, "fin1": gain_end,
    }
    for m in range(2):
        events |= {
            f"act{m}": functools.partial(gelu, m),
            f"gpre{m}": functools.partial(gradient, m),
            f"out{m}.cmp": functools.partial(out_compute, m),
            f"gn{m}.cmp": functools.partial(gn_compute, m),
        }
    steps = {}
    for name, one in gather.items():
        steps[f"{name}.own"] = functools.partial(own_part, name)
        steps[f"{name}.end"] = functools.partial(end_part, name)
        steps[f"{name}.cmp"] = functools.partial(compute, name)
        steps[f"{name}.rson"] = row_sum[name].onward
        steps[f"{name}.near"], steps[f"{name}.far"] = one.near, one.far
        for i in range(4):
            steps[f"{name}.on{i}"] = functools.partial(one.onward, i)
    for name, one in plane_sum.items():
        for step in ("on", "cross", "near", "end"):
            steps[f"{name}.{step}"] = getattr(one, {"on": "onward"}.get(step, step))
    for name in ORDER:
        if name in events:
            events.pop(name)()
        elif name.endswith(".on") and name[:-3] in row_gather:
            row_gather[name[:-3]].onward()
        else:
            steps.pop(name)()
    assert not events and not steps

    for one in started:
        one.wait_send()
    for one in (c["swC"], c["swT"], *(plane.m for plane in plane_sum.values())):
        mirrored_sent(one)


def scratch():
    def buf(*shape, kind=BF16):
        return pltpu.VMEM(shape, kind)

    def twice(*shape, kind=BF16):
        return [buf(*shape, kind=kind), buf(*shape, kind=kind)]

    return [
        buf(CHUNK, PAIR), buf(PAIR, CHUNK),
        buf(SHARE, ROWS, kind=F32), buf(11, 8, ROWS, kind=F32),
        buf(4, 8, SHARE, kind=F32),
        buf(5, 8, SHARE, kind=F32), buf(4, 8, GROUP, kind=F32), buf(4, 8, PAIR, kind=F32),
        buf(2, PART, PAIR, kind=F32), buf(2, PART, PAIR, kind=F32),
        buf(HALF, 128, kind=F32), buf(10, 8, HALF, kind=F32),
        *twice(ROWS, SHARE), *twice(HALF, SHARE), *twice(HALF, GROUP),
        *twice(4, 4, HALF, GROUP), *twice(8 * PART, CHUNK),
        *twice(2, 4, PART, PAIR, kind=F32), *twice(2, 4, PART, PAIR),
        *twice(2, 2, PART // 2, PAIR), *twice(2, 2, PART, PAIR),
        *twice(2, 4, PART, PAIR),
        *twice(2, 4, 4, PART, GROUP),
        *twice(2, 2, 4, PART // 2, GROUP), *twice(2, 2, 4, PART, GROUP),
        *twice(2, 4, PART, GROUP), *twice(2, 2, PART // 2, GROUP),
        *twice(2, 2, PART, GROUP), *twice(2, PART, GROUP, kind=F32),
        *twice(2, PART, GROUP), *twice(HALF, SHARE), *twice(HALF, SHARE),
        buf(HID, CHUNK, kind=F32), buf(HID, CHUNK, kind=F32), buf(HID, CHUNK, kind=F32),
        buf(CHUNK, HID, kind=F32), buf(CHUNK, HID, kind=F32), buf(CHUNK, HID, kind=F32),
        pltpu.SemaphoreType.DMA((COPIES,)),
        pltpu.SemaphoreType.DMA((COPIES,)),
        pltpu.SemaphoreType.DMA((2,)),
    ]


def deliver(*refs):
    sources, landings, sem = refs[:5], refs[5:10], refs[10]
    moves = [
        pltpu.make_async_copy(source, landing, sem.at[i])
        for i, (source, landing) in enumerate(zip(sources, landings))
    ]
    for move in moves:
        move.start()
    for move in moves:
        move.wait()


def body(tokens, norm_gain, inner_weight, outer_weight, cotangent):
    vmem, anywhere = pl.BlockSpec(memory_space=pltpu.VMEM), pl.BlockSpec(memory_space=pl.ANY)
    shapes = [
        ((SHARE, ROWS), BF16), ((SHARE, ROWS), BF16), ((1, SHARE), F32),
        ((CHUNK, HID), F32), ((HID, CHUNK), F32),
    ]
    outs = pl.pallas_call(
        kernel,
        out_shape=[pltpu.VMEM(shape, kind) for shape, kind in shapes],
        in_specs=[vmem, vmem, anywhere, anywhere, vmem],
        out_specs=[vmem] * 5,
        scratch_shapes=scratch(),
        compiler_params=pltpu.CompilerParams(
            collective_id=0, has_side_effects=True, vmem_limit_bytes=VMEM_BYTES
        ),
        name="mlp_block",
    )(tokens.T, norm_gain, inner_weight, outer_weight, cotangent.T)
    branch_out, grad_tokens, grad_gain, grad_inner, grad_outer = pl.pallas_call(
        deliver,
        out_shape=[jax.ShapeDtypeStruct(shape, kind) for shape, kind in shapes],
        in_specs=[vmem] * 5,
        out_specs=[anywhere] * 5,
        scratch_shapes=[pltpu.SemaphoreType.DMA((5,))],
        name="deliver",
    )(*outs)
    return (branch_out.T, grad_tokens.T, grad_gain.reshape(SHARE), grad_inner, grad_outer)


def solution(mesh):
    return jax.shard_map(
        body,
        mesh=mesh,
        in_specs=(P("row", "col"), P("col"), P("row", "col"), P("col", "row"), P("row", "col")),
        out_specs=(P("row", "col"), P("row", "col"), P("col"), P("row", "col"), P("col", "row")),
        check_vma=False,
    )
```

```python
import functools

import jax
import jax.numpy as jnp
from jax import lax
from jax.experimental import pallas as pl
from jax.experimental.pallas import tpu as pltpu
from jax.sharding import PartitionSpec as P

inv_sqrt_two = 0.7071067811865476
inv_sqrt_tau = 0.3989422804014327
MESH = pl.DeviceIdType.MESH
BF16 = jnp.bfloat16
F32 = jnp.float32

ROWS, SHARE = 384, 192
HALF, PARTS = 192, 3
PART = HALF // PARTS
GROUP, CHUNK = 384, 1536
HID, PAIR = 384, 768
FEATURES = 6144
COPIES = 360
VMEM_BYTES = 54 * 1024 * 1024
FIRST_COT, FIRST_PART = 2, 2


def gelu_parts(hidden_pre):
    cumulative = 0.5 * (1.0 + lax.erf(hidden_pre * inv_sqrt_two))
    density = jnp.exp(-0.5 * hidden_pre * hidden_pre) * inv_sqrt_tau
    return (hidden_pre * cumulative, cumulative + hidden_pre * density)


def dot_nn(left, right):
    return jnp.dot(left, right, preferred_element_type=F32)


def dot_nt(left, right):
    return lax.dot_general(
        left, right, (((1,), (1,)), ((), ())), preferred_element_type=F32
    )


def dot_tn(left, right):
    return lax.dot_general(
        left, right, (((0,), (0,)), ((), ())), preferred_element_type=F32
    )


def turn(index, by):
    return lax.rem(index + (by % 4), 4)


def merge_moments(parts, count):
    mean = sum(p[0:1] for p in parts) * (1.0 / len(parts))
    second = sum(p[1:2] + count * (p[0:1] - mean) ** 2 for p in parts)
    return jnp.concatenate([mean, second, jnp.zeros((6, ROWS), F32)], axis=0)


def kernel(
    tok_hbm, gain_ref, w_in, w_out, cot_hbm,
    branch_ref, gtok_ref, ggain_ref, ginner_ref, gouter_ref,
    tok_ref, cot_ref, w1, w2, unit, stat, ggbuf, gz, gx, gy, hidden, slope, sums, ms, nat_tok, nat_cot,
    mrg_tok, mrg_cot, own_tok, own_cot, raw_tok, g_tok, g_cot, n_tok, n_cot,
    hf_tok, hf_cot, hb_tok, hb_cot, y1_tok, y1_cot, y2_tok, y2_cot,
    act, gpre,
    pb_out, pb_gn, r1_out, r1_gn, r2_out, r2_gn, s_out, s_gn, r4_out, r4_gn,
    f_out, f_gn, o_out, o_gn, c_out, c_gn, d_out, d_gn,
    go_own, go_send, go_recv, gi_own, gi_send, gi_recv,
    send_sem, recv_sem, local_sem,
):
    y = lax.axis_index("row")
    col = lax.axis_index("col")
    z, x, q = col // 8, lax.rem(col // 2, 4), lax.rem(col, 2)
    p = 1 - q
    a0, b0 = p * x + q * z, p * z + q * x
    am, ap, a2 = turn(a0, -1), turn(a0, 1), turn(a0, 2)
    bm, bp, b2 = turn(b0, -1), turn(b0, 1), turn(b0, 2)
    ym, yp, y2 = turn(y, -1), turn(y, 1), turn(y, 2)
    first, second = q == 0, y != z

    def device(yy, zz, xx, qq):
        return (yy, zz * 8 + xx * 2 + qq)

    def on_a(by):
        return device(y, lax.rem(z + q * (by % 4), 4), lax.rem(x + p * (by % 4), 4), q)

    def on_b(by):
        return device(y, lax.rem(z + p * (by % 4), 4), lax.rem(x + q * (by % 4), 4), q)

    def on_y(by):
        return device(turn(y, by), z, x, q)

    mate = device(y, z, x, p)
    mirror = device(z, y, x, q)
    started, count = [], [0]

    def copy(src, dst, to):
        at = count[0]
        count[0] += 1
        return pltpu.make_async_remote_copy(
            src_ref=src, dst_ref=dst, send_sem=send_sem.at[at], recv_sem=recv_sem.at[at],
            device_id=to, device_id_type=MESH,
        )

    def send(src, dst, to):
        c = copy(src, dst, to)
        c.start()
        started.append(c)
        return c

    def left(c):
        c.wait_send()
        started[:] = [other for other in started if other is not c]

    def rows_of(half):
        return pl.ds(pl.multiple_of(half * HALF, HALF), HALF)

    top, bottom = pl.ds(0, PART // 2), pl.ds(PART // 2, PART // 2)

    barrier = pltpu.get_barrier_semaphore()
    others = [mate] + [on(by) for on in (on_a, on_b, on_y) for by in (1, 2, 3)]
    for other in others:
        pl.semaphore_signal(barrier, inc=1, device_id=other, device_id_type=MESH)

    @pl.when(second)
    def _():
        pl.semaphore_signal(barrier, inc=1, device_id=mirror, device_id_type=MESH)

    hid_own = pl.ds(pl.multiple_of(q * HID, HID), HID)
    local_in = pltpu.make_async_copy(w_in, w1.at[:, hid_own], local_sem.at[0])
    local_out = pltpu.make_async_copy(w_out, w2.at[hid_own], local_sem.at[1])
    local_tok = pltpu.make_async_copy(tok_hbm, tok_ref, local_sem.at[2])
    local_cot = pltpu.make_async_copy(cot_hbm, cot_ref, local_sem.at[3])
    local_cot.start()
    local_tok.start()
    local_out.start()
    local_in.start()
    local_cot.wait()
    nat_cot[...] = cot_ref[...].astype(F32).T.astype(BF16)
    local_tok.wait()
    nat_tok[...] = tok_ref[...].astype(F32).T.astype(BF16)

    values = tok_ref[...].astype(F32)
    own_mean = jnp.sum(values, axis=0, keepdims=True) * (1.0 / SHARE)
    own_second = jnp.sum((values - own_mean) ** 2, axis=0, keepdims=True)
    stat[0] = jnp.concatenate([own_mean, own_second, jnp.zeros((6, ROWS), F32)], axis=0)
    gz[z] = jnp.broadcast_to(gain_ref[...].astype(F32).reshape(1, SHARE), (8, SHARE))

    @pl.when(second)
    def _():
        pl.semaphore_wait(barrier, len(others) + 1)

    @pl.when(jnp.logical_not(second))
    def _():
        pl.semaphore_wait(barrier, len(others))

    def joined(own, other):
        return jnp.where(
            first,
            jnp.concatenate([own, other], axis=1),
            jnp.concatenate([other, own], axis=1),
        )

    def mirrored(piece, landing, at_home):
        c = copy(piece, landing, mirror)

        @pl.when(second)
        def _():
            c.start()

        @pl.when(jnp.logical_not(second))
        def _():
            at_home[...] = piece[...]

        return c

    def mirrored_wait(c):
        @pl.when(second)
        def _():
            c.wait_recv()

    def mirrored_sent(c):
        @pl.when(second)
        def _():
            c.wait_send()

    b_there, a_there = p * y + q * x, p * x + q * y

    class Gather:
        def __init__(self, g, part):
            self.g, self.part = g, part

        def at(self, b, a, side=None):
            rows = {None: (0, PART), 0: (0, PART // 2), 1: (PART // 2, PART // 2)}[side]
            return self.g.at[b, a, pl.ds(self.part * PART + rows[0], rows[1])]

        def own(self):
            home = self.at(b0, a0)
            self.a = [send(home, home, on_a(by)) for by in (1, -1, 2)]
            self.b, self.fb = {0: self.both(home)}, []

        def both(self, piece):
            return send(piece, piece, on_b(1)), send(piece, piece, on_b(-1))

        def near(self):
            self.a[0].wait_recv()
            self.b[1] = self.both(self.at(b0, am))
            self.a[1].wait_recv()
            self.b[2] = self.both(self.at(b0, ap))

        def far(self):
            self.a[2].wait_recv()
            self.b[3] = self.both(self.at(b0, a2))

        def onward(self, i):
            a = (a0, am, ap, a2)[i]
            self.b[i][0].wait_recv()
            left = self.at(bm, a, 0)
            up = send(left, left, on_b(1))
            self.b[i][1].wait_recv()
            right = self.at(bp, a, 1)
            down = send(right, right, on_b(-1))
            self.fb.append((up, down))

        def end(self, n):
            for up, down in self.fb:
                up.wait_recv()
                down.wait_recv()
            rows = pl.ds(self.part * PART, PART)
            for j in range(4):
                for s in range(4):
                    to = pl.ds((self.part * 4 + j) * PART, PART)
                    n[to, s * GROUP : (s + 1) * GROUP] = self.g[p * j + q * s, p * s + q * j, rows]

    class RowSum:
        def __init__(self, hf, hb, r1, r2, part):
            self.hf, self.hb = hf.at[part], hb.at[part]
            self.r1, self.r2 = r1.at[part], r2.at[part]

        def compute(self, value):
            hf, hb, r1, r2 = self.hf, self.hb, self.r1, self.r2
            for j in range(4):
                block = value[j * PART : (j + 1) * PART]
                hf[j] = block
                hb[j] = block.astype(BF16)
            self.up1 = send(hb.at[y2, top], r1.at[0], on_y(1))
            self.down1 = send(hb.at[y2, bottom], r1.at[1], on_y(-1))
            self.up2 = send(hb.at[yp, bottom], r2.at[0, bottom], on_y(1))
            self.down2 = send(hb.at[ym, top], r2.at[1, top], on_y(-1))

        def onward(self):
            hf, hb, r1, r2 = self.hf, self.hb, self.r1, self.r2
            self.up1.wait_recv()
            hb[yp, top] = (hf[yp, top] + r1[0].astype(F32)).astype(BF16)
            self.up3 = send(hb.at[yp, top], r2.at[0, top], on_y(1))
            self.down1.wait_recv()
            hb[ym, bottom] = (hf[ym, bottom] + r1[1].astype(F32)).astype(BF16)
            self.down3 = send(hb.at[ym, bottom], r2.at[1, bottom], on_y(-1))

        def end(self):
            for c in (self.up2, self.up3, self.down2, self.down3):
                c.wait_recv()
            return self.hf[y] + self.r2[0].astype(F32) + self.r2[1].astype(F32)

    class RowGather:
        def __init__(self, g, part, block):
            g = self.g = g.at[part]
            g[y] = block
            self.up, self.down = send(g.at[y], g.at[y], on_y(1)), send(g.at[y], g.at[y], on_y(-1))

        def onward(self):
            g = self.g
            self.up.wait_recv()
            self.fup = send(g.at[ym, top], g.at[ym, top], on_y(1))
            self.down.wait_recv()
            self.fdown = send(g.at[yp, bottom], g.at[yp, bottom], on_y(-1))

        def end(self):
            self.fup.wait_recv()
            self.fdown.wait_recv()
            return self.g[...].reshape(4 * PART, PAIR)

    class PlaneSum:
        def __init__(self, pb, r1, r2, s, r4, f, o, part):
            self.pb, self.r1, self.r2, self.s = pb.at[part], r1.at[part], r2.at[part], s.at[part]
            self.r4, self.f, self.o = r4.at[part], f.at[part], o.at[part]

        def compute(self, product):
            pb, r1, r2 = self.pb, self.r1, self.r2
            for wide in range(2):
                value = product(wide * 2 * GROUP, 2 * GROUP)
                for j in range(4):
                    for t in range(2):
                        s = wide * 2 + t
                        pb[p * j + q * s, p * s + q * j] = value[
                            j * PART : (j + 1) * PART, t * GROUP : (t + 1) * GROUP
                        ].astype(BF16)
            self.up1 = send(pb.at[b2, :, top], r1.at[0], on_b(1))
            self.down1 = send(pb.at[b2, :, bottom], r1.at[1], on_b(-1))
            self.up2 = send(pb.at[bp, :, bottom], r2.at[0, :, bottom], on_b(1))
            self.down2 = send(pb.at[bm, :, top], r2.at[1, :, top], on_b(-1))

        def onward(self):
            pb, r1, r2 = self.pb, self.r1, self.r2
            self.up1.wait_recv()
            pb[bp, :, top] = (pb[bp, :, top].astype(F32) + r1[0].astype(F32)).astype(BF16)
            self.up3 = send(pb.at[bp, :, top], r2.at[0, :, top], on_b(1))
            self.down1.wait_recv()
            pb[bm, :, bottom] = (pb[bm, :, bottom].astype(F32) + r1[1].astype(F32)).astype(BF16)
            self.down3 = send(pb.at[bm, :, bottom], r2.at[1, :, bottom], on_b(-1))

        def cross(self):
            pb, r2, s, r4 = self.pb, self.r2, self.s, self.r4
            for c in (self.up2, self.down2, self.up3, self.down3):
                c.wait_recv()

            def summed(a):
                return pb[b0, a].astype(F32) + r2[0, a].astype(F32) + r2[1, a].astype(F32)

            self.a = []
            for slot, (to, by) in enumerate(((a2, 2), (ap, 1), (am, -1))):
                s[to] = summed(to).astype(BF16)
                self.a.append(send(s.at[to], r4.at[slot], on_a(by)))
            self.f[...] = summed(a0)

        def end(self):
            for c in self.a:
                c.wait_recv()
            total = self.f[...] + sum(self.r4[slot].astype(F32) for slot in range(3))
            self.s[a0] = total.astype(BF16)
            self.m = mirrored(self.s.at[a0], self.o, self.o)

    give, keep = rows_of(p), rows_of(q)
    gain_column, moment_columns = [], []
    cot = [Gather(g_cot, m) for m in range(PARTS)]
    tok = [Gather(g_tok, m) for m in range(PARTS)]
    cot_sum = [RowSum(hf_cot, hb_cot, y1_cot, y2_cot, m) for m in range(PARTS)]
    tok_sum = [RowSum(hf_tok, hb_tok, y1_tok, y2_tok, m) for m in range(PARTS)]
    out_sum = [
        PlaneSum(pb_out, r1_out, r2_out, s_out, r4_out, f_out, o_out, m) for m in range(PARTS)
    ]
    gn_sum = [PlaneSum(pb_gn, r1_gn, r2_gn, s_gn, r4_gn, f_gn, o_gn, m) for m in range(PARTS)]
    cot_swaps, tok_swaps, act_gather, gpre_gather, c = {}, {}, {}, {}, {}

    def three(src, buffer, first_slot, on):
        return [send(src, buffer.at[first_slot + by - 1], on(by)) for by in (1, 2, 3)]

    def arrived(copies):
        for one in copies:
            one.wait_recv()

    def on_z(by):
        return device(y, turn(z, by), x, q)

    def on_x(by):
        return device(y, z, turn(x, by), q)

    def start():
        c["mrg_cot"] = send(nat_cot.at[give], mrg_cot, mate)
        c["mrg_tok"] = send(nat_tok.at[give], mrg_tok, mate)
        c["st0"] = send(stat.at[0], stat.at[1], mate)
        c["w2"] = send(w_out, w2.at[hid_own], mate)
        c["w1"] = send(w_in, w1.at[:, hid_own], mate)
        c["gz"] = [send(gz.at[z], gz.at[z], on_z(by)) for by in (1, 2, 3)]

    def cot_merge():
        c["mrg_cot"].wait_recv()
        own_cot[...] = joined(nat_cot[keep].astype(F32), mrg_cot[...].astype(F32)).astype(BF16)

    def cot_swap(m):
        rows = pl.ds(m * PART, PART)
        there, here = g_cot.at[b_there, a_there, rows], g_cot.at[b0, a0, rows]
        cot_swaps[m] = mirrored(own_cot.at[rows], there, here)

    def moments_cores():
        c["st0"].wait_recv()
        stat[2] = merge_moments([stat[0], stat[1]], SHARE)
        c["st1"] = three(stat.at[2], stat, 3, on_a)

    def moments_a():
        arrived(c["st1"])
        stat[6] = merge_moments([stat[2 + by] for by in range(4)], 2 * SHARE)
        c["st2"] = three(stat.at[6], stat, 7, on_b)

    def moments_b():
        arrived(c["st2"])
        moments = merge_moments([stat[6 + by] for by in range(4)], 8 * SHARE)
        inv_std = lax.rsqrt(moments[1:2] * (1.0 / FEATURES) + 1e-06)
        stat[10] = jnp.concatenate([moments[0:1], inv_std, jnp.zeros((6, ROWS), F32)], axis=0)
        c["stM"] = mirrored(stat.at[10], stat.at[11], stat.at[11])

    def own_unit():
        unit[...] = (tok_ref[...].astype(F32) - stat[10, 0:1]) * stat[10, 1:2]
        gain_values = gain_ref[...].astype(F32).reshape(1, SHARE)
        gain_column.append(jnp.broadcast_to(gain_values, (128, SHARE)).T[:, 0:1])

    def tok_merge():
        c["mrg_tok"].wait_recv()
        own_tok[...] = joined(nat_tok[keep].astype(F32), mrg_tok[...].astype(F32)).astype(BF16)

    def tok_swap(m):
        rows = pl.ds(m * PART, PART)
        tok_swaps[m] = mirrored(own_tok.at[rows], raw_tok.at[rows], raw_tok.at[rows])

    def normalise(m):
        if not moment_columns:
            mirrored_wait(c["stM"])
            both = jnp.where(first, stat[11, :, 0:HALF], stat[11, :, HALF:ROWS])
            both = jnp.concatenate([both, jnp.zeros((120, HALF), F32)], axis=0).T
            moment_columns.extend([both[:, 0:1], both[:, 1:2]])
        rows = slice(m * PART, (m + 1) * PART)
        mean, inv_std = (column[rows] for column in moment_columns)
        unit_rows = (raw_tok[rows].astype(F32) - mean) * inv_std
        g_tok[b0, a0, rows] = (unit_rows * gx[x, 0:1]).astype(BF16)

    def gain_z():
        arrived(c["gz"])
        c["gm"] = send(gz.at[y], gz.at[4], mate)

    def gain_cores():
        c["gm"].wait_recv()
        gx[x] = joined(gz[y], gz[4])
        c["gx"] = [send(gx.at[x], gx.at[x], on_x(by)) for by in (1, 2, 3)]

    def gain_x():
        arrived(c["gx"])
        local_in.wait()
        c["w1"].wait_recv()
        gy[0] = sum(
            dot_nn(gx[s].astype(BF16), w1[s * GROUP : (s + 1) * GROUP]) for s in range(4)
        )
        c["gy"] = three(gy.at[0], gy, 1, on_y)

    def part_rows(m):
        return pl.ds(m * 4 * PART, 4 * PART)

    def cot_own(m):
        mirrored_wait(cot_swaps[m])
        cot[m].own()

    def tok_own(m):
        mirrored_wait(tok_swaps[m])
        normalise(m)
        tok[m].own()

    def cot_compute(m):
        if m == FIRST_COT:
            local_out.wait()
            c["w2"].wait_recv()
        cot_sum[m].compute(dot_nt(n_cot[part_rows(m)], w2[...]))

    def tok_compute(m):
        tok_sum[m].compute(dot_nn(n_tok[part_rows(m)], w1[...]))

    def gelu(m):
        hidden_pre = tok_sum[m].end()
        gelu_value, slope[m] = gelu_parts(hidden_pre)
        hidden[m] = hidden_pre
        act_gather[m] = RowGather(act, m, gelu_value.astype(BF16))

    def gradient(m):
        if m == FIRST_PART:
            arrived(c["gy"])
        grad_pre = (cot_sum[m].end() * slope[m]).astype(BF16)
        gpre_gather[m] = RowGather(gpre, m, grad_pre)
        grad_pre = grad_pre.astype(F32)
        gain_row = (gy[0] + gy[1] + gy[2] + gy[3])[0:1]
        one = jnp.sum(grad_pre * gain_row, axis=1, keepdims=True)
        two = jnp.sum(grad_pre * hidden[m], axis=1, keepdims=True)
        lane = lax.broadcasted_iota(jnp.int32, (PART, 128), 1)
        sums[m * PART : (m + 1) * PART] = jnp.where(lane == 0, one, two)

    def means_cores():
        ms[0] = sums[...].T[0:8]
        c["ms0"] = three(ms.at[0], ms, 1, on_a)

    def means_a():
        arrived(c["ms0"])
        ms[4] = ms[0] + ms[1] + ms[2] + ms[3]
        c["ms1"] = three(ms.at[4], ms, 5, on_b)

    def means_b():
        arrived(c["ms1"])
        ms[8] = (ms[4] + ms[5] + ms[6] + ms[7]) * (1.0 / FEATURES)
        c["ms2"] = send(ms.at[8], ms.at[9], mate)

    def out_compute(m):
        block = act_gather[m].end()
        out_sum[m].compute(lambda at, wide: dot_nn(block, w2[:, at : at + wide]))

    def gn_compute(m):
        block = gpre_gather[m].end()
        gn_sum[m].compute(lambda at, wide: dot_nt(block, w1[at : at + wide]))

    def by_hidden(who):
        return pl.ds(pl.multiple_of(who * HID, HID), HID)

    def grad_outer(who, into):
        block = act[:, :, :, by_hidden(who)].reshape(4 * HALF, HID)
        into[...] = dot_tn(block, n_cot[...])

    def grad_inner(who, into):
        block = gpre[:, :, :, by_hidden(who)].reshape(4 * HALF, HID)

        def step(t, _):
            at = pl.ds(pl.multiple_of(t * GROUP, GROUP), GROUP)
            into[at] = dot_tn(n_tok[:, at], block)
            return 0

        lax.fori_loop(0, 4, step, 0)

    def outer_send():
        grad_outer(p, go_send)
        c["go"] = send(go_send, go_recv, mate)

    def inner_send():
        grad_inner(p, gi_send)
        c["gi"] = send(gi_send, gi_recv, mate)

    def outer_add():
        c["go"].wait_recv()
        gouter_ref[...] = go_own[...] + go_recv[...]

    def inner_add():
        c["gi"].wait_recv()
        ginner_ref[...] = gi_own[...] + gi_recv[...]

    def split(sums, o, to_mate, landing):
        for one in sums:
            mirrored_wait(one.m)
        piece = o[...].reshape(HALF, GROUP).astype(F32)
        low, high = piece[:, 0:SHARE], piece[:, SHARE:GROUP]
        to_mate[...] = jnp.where(first, high, low).astype(BF16)
        return jnp.where(first, low, high).astype(BF16), send(to_mate, landing, mate)

    def out_split():
        left(c["mrg_cot"])
        nat_cot[keep], c["out"] = split(out_sum, o_out, c_out, d_out)

    def gn_split():
        left(c["mrg_tok"])
        nat_tok[keep], c["gn"] = split(gn_sum, o_gn, c_gn, d_gn)

    def out_end():
        c["out"].wait_recv()
        nat_cot[give] = d_out[...]
        branch_ref[...] = nat_cot[...].astype(F32).T.astype(BF16)

    def gn_end():
        c["gn"].wait_recv()
        nat_tok[give] = d_gn[...]
        unit_rows = unit[...]
        grad_normed = nat_tok[...].astype(F32).T
        gain_part = jnp.sum(grad_normed * unit_rows, axis=1, keepdims=True)
        ggbuf[0] = jnp.broadcast_to(gain_part, (SHARE, 128)).T[0:8]
        c["gg"] = three(ggbuf.at[0], ggbuf, 1, on_y)
        c["ms2"].wait_recv()
        means = joined(ms[8], ms[9])
        grad_hat = grad_normed * gain_column[0]
        gtok_ref[...] = (
            stat[10, 1:2] * (grad_hat - means[0:1] - unit_rows * means[1:2])
        ).astype(BF16)

    def gain_end():
        arrived(c["gg"])
        ggain_ref[...] = (ggbuf[0] + ggbuf[1] + ggbuf[2] + ggbuf[3])[0:1]

    start()
    cot_merge()
    cot_swap(2)
    cot_swap(0)
    cot_swap(1)
    gain_z()
    moments_cores()
    tok_merge()
    tok_swap(2)
    tok_swap(1)
    tok_swap(0)
    moments_a()
    cot_own(2)
    gain_cores()
    cot_own(0)
    moments_b()
    cot[2].near()
    own_unit()
    cot[2].far()
    cot[2].onward(0)
    gain_x()
    cot[0].near()
    cot[0].onward(0)
    cot[0].far()
    cot[2].onward(1)
    cot[2].onward(2)
    cot[2].onward(3)
    tok_own(2)
    cot[0].onward(1)
    cot[0].onward(2)
    cot[0].onward(3)
    tok_own(0)
    cot[2].end(n_cot)
    cot_compute(2)
    tok[2].far()
    tok[2].near()
    tok[2].onward(0)
    cot[0].end(n_cot)
    cot_compute(0)
    tok[0].near()
    tok[0].far()
    tok[0].onward(0)
    cot_sum[2].onward()
    tok[2].onward(3)
    tok[2].onward(1)
    tok[2].onward(2)
    tok[0].onward(1)
    cot_sum[0].onward()
    tok[0].onward(2)
    tok[0].onward(3)
    tok[2].end(n_tok)
    tok_compute(2)
    tok[0].end(n_tok)
    tok_compute(0)
    cot_own(1)
    tok_sum[2].onward()
    tok_own(1)
    cot[1].near()
    tok_sum[0].onward()
    gelu(2)
    gradient(2)
    cot[1].onward(0)
    tok[1].near()
    tok[1].far()
    tok[1].onward(0)
    cot[1].onward(1)
    cot[1].onward(2)
    gelu(0)
    gradient(0)
    cot[1].far()
    act_gather[2].onward()
    tok[1].onward(1)
    tok[1].onward(2)
    tok[1].onward(3)
    cot[1].onward(3)
    gpre_gather[2].onward()
    tok[1].end(n_tok)
    tok_compute(1)
    act_gather[0].onward()
    cot[1].end(n_cot)
    cot_compute(1)
    gpre_gather[0].onward()
    out_compute(2)
    gn_compute(2)
    tok_sum[1].onward()
    out_compute(0)
    cot_sum[1].onward()
    out_sum[2].onward()
    gn_compute(0)
    gelu(1)
    out_sum[0].onward()
    gradient(1)
    means_cores()
    out_sum[2].cross()
    gn_sum[0].onward()
    gn_sum[2].onward()
    act_gather[1].onward()
    out_sum[0].cross()
    out_sum[2].end()
    gpre_gather[1].onward()
    gn_sum[0].cross()
    gn_sum[2].cross()
    out_compute(1)
    gn_compute(1)
    out_sum[0].end()
    gn_sum[0].end()
    outer_send()
    gn_sum[1].onward()
    gn_sum[2].end()
    out_sum[1].onward()
    inner_send()
    gn_sum[1].cross()
    grad_inner(q, gi_own)
    out_sum[1].cross()
    gn_sum[1].end()
    means_a()
    grad_outer(q, go_own)
    out_sum[1].end()
    outer_add()
    means_b()
    gn_split()
    gn_end()
    out_split()
    inner_add()
    out_end()
    gain_end()

    for one in started:
        one.wait_send()
    swaps = [*cot_swaps.values(), *tok_swaps.values(), c["stM"]]
    for one in (*swaps, *(plane.m for plane in out_sum + gn_sum)):
        mirrored_sent(one)


def scratch():
    def buf(*shape, kind=BF16):
        return pltpu.VMEM(shape, kind)

    def twice(*shape, kind=BF16):
        return [buf(*shape, kind=kind), buf(*shape, kind=kind)]

    return [
        *twice(SHARE, ROWS), buf(CHUNK, PAIR), buf(PAIR, CHUNK),
        buf(SHARE, ROWS, kind=F32), buf(12, 8, ROWS, kind=F32),
        buf(4, 8, SHARE, kind=F32),
        buf(5, 8, SHARE, kind=F32), buf(4, 8, GROUP, kind=F32), buf(4, 8, PAIR, kind=F32),
        buf(PARTS, PART, PAIR, kind=F32), buf(PARTS, PART, PAIR, kind=F32),
        buf(HALF, 128, kind=F32), buf(10, 8, HALF, kind=F32),
        *twice(ROWS, SHARE), *twice(HALF, SHARE), *twice(HALF, GROUP), buf(HALF, GROUP),
        *twice(4, 4, HALF, GROUP), *twice(4 * HALF, CHUNK),
        *twice(PARTS, 4, PART, PAIR, kind=F32), *twice(PARTS, 4, PART, PAIR),
        *twice(PARTS, 2, PART // 2, PAIR), *twice(PARTS, 2, PART, PAIR),
        *twice(PARTS, 4, PART, PAIR),
        *twice(PARTS, 4, 4, PART, GROUP),
        *twice(PARTS, 2, 4, PART // 2, GROUP), *twice(PARTS, 2, 4, PART, GROUP),
        *twice(PARTS, 4, PART, GROUP), *twice(PARTS, 3, PART, GROUP),
        *twice(PARTS, PART, GROUP, kind=F32),
        *twice(PARTS, PART, GROUP), *twice(HALF, SHARE), *twice(HALF, SHARE),
        buf(HID, CHUNK, kind=F32), buf(HID, CHUNK, kind=F32), buf(HID, CHUNK, kind=F32),
        buf(CHUNK, HID, kind=F32), buf(CHUNK, HID, kind=F32), buf(CHUNK, HID, kind=F32),
        pltpu.SemaphoreType.DMA((COPIES,)),
        pltpu.SemaphoreType.DMA((COPIES,)),
        pltpu.SemaphoreType.DMA((4,)),
    ]


def body(tokens, norm_gain, inner_weight, outer_weight, cotangent):
    vmem, anywhere = pl.BlockSpec(memory_space=pltpu.VMEM), pl.BlockSpec(memory_space=pl.ANY)
    shapes = [
        ((SHARE, ROWS), BF16), ((SHARE, ROWS), BF16), ((1, SHARE), F32),
        ((CHUNK, HID), F32), ((HID, CHUNK), F32),
    ]
    branch_out, grad_tokens, grad_gain, grad_inner, grad_outer = pl.pallas_call(
        kernel,
        out_shape=[pltpu.VMEM(shape, kind) for shape, kind in shapes],
        in_specs=[anywhere, vmem, anywhere, anywhere, anywhere],
        out_specs=[vmem] * 5,
        scratch_shapes=scratch(),
        compiler_params=pltpu.CompilerParams(
            collective_id=0, has_side_effects=True, vmem_limit_bytes=VMEM_BYTES
        ),
        name="mlp_block",
    )(tokens.T, norm_gain, inner_weight, outer_weight, cotangent.T)
    return (branch_out.T, grad_tokens.T, grad_gain.reshape(SHARE), grad_inner, grad_outer)


def solution(mesh):
    return jax.shard_map(
        body,
        mesh=mesh,
        in_specs=(P("row", "col"), P("col"), P("row", "col"), P("col", "row"), P("row", "col")),
        out_specs=(P("row", "col"), P("row", "col"), P("col"), P("row", "col"), P("col", "row")),
        check_vma=False,
    )
```

```python
import functools

import jax
import jax.numpy as jnp
from jax import lax
from jax.experimental import pallas as pl
from jax.experimental.pallas import tpu as pltpu
from jax.sharding import PartitionSpec as P

inv_sqrt_two = 0.7071067811865476
inv_sqrt_tau = 0.3989422804014327
MESH = pl.DeviceIdType.MESH
BF16 = jnp.bfloat16
F32 = jnp.float32

ROWS, SHARE = 384, 192
HALF, PARTS = 192, 3
PART = HALF // PARTS
GROUP, CHUNK = 384, 1536
HID, PAIR = 384, 768
FEATURES = 6144
COPIES = 360
VMEM_BYTES = 54 * 1024 * 1024
FIRST_COT, FIRST_PART = 2, 2


def gelu_parts(hidden_pre):
    cumulative = 0.5 * (1.0 + lax.erf(hidden_pre * inv_sqrt_two))
    density = jnp.exp(-0.5 * hidden_pre * hidden_pre) * inv_sqrt_tau
    return (hidden_pre * cumulative, cumulative + hidden_pre * density)


def dot_nn(left, right):
    return jnp.dot(left, right, preferred_element_type=F32)


def dot_nt(left, right):
    return lax.dot_general(
        left, right, (((1,), (1,)), ((), ())), preferred_element_type=F32
    )


def dot_tn(left, right):
    return lax.dot_general(
        left, right, (((0,), (0,)), ((), ())), preferred_element_type=F32
    )


def turn(index, by):
    return lax.rem(index + (by % 4), 4)


def merge_moments(parts, count):
    mean = sum(p[0:1] for p in parts) * (1.0 / len(parts))
    second = sum(p[1:2] + count * (p[0:1] - mean) ** 2 for p in parts)
    return jnp.concatenate([mean, second, jnp.zeros((6, ROWS), F32)], axis=0)


def kernel(
    tok_hbm, gain_ref, w_in, w_out, cot_hbm,
    branch_ref, gtok_ref, ggain_ref, ginner_ref, gouter_ref,
    tok_ref, cot_ref, w1, w2, unit, stat, ggbuf, gz, gx, gy, hidden, slope, sums, ms, nat_tok, nat_cot,
    mrg_tok, mrg_cot, own_tok, own_cot, raw_tok, g_tok, g_cot, n_tok, n_cot,
    hf_tok, hf_cot, hb_tok, hb_cot, y1_tok, y1_cot, y2_tok, y2_cot,
    act, gpre,
    pb_out, pb_gn, r1_out, r1_gn, r2_out, r2_gn, s_out, s_gn, r4_out, r4_gn,
    f_out, f_gn, o_out, o_gn, c_out, c_gn, d_out, d_gn,
    go_own, go_send, go_recv, gi_own, gi_send, gi_recv,
    send_sem, recv_sem, local_sem,
):
    y = lax.axis_index("row")
    col = lax.axis_index("col")
    z, x, q = col // 8, lax.rem(col // 2, 4), lax.rem(col, 2)
    p = 1 - q
    a0, b0 = p * x + q * z, p * z + q * x
    am, ap, a2 = turn(a0, -1), turn(a0, 1), turn(a0, 2)
    bm, bp, b2 = turn(b0, -1), turn(b0, 1), turn(b0, 2)
    ym, yp, y2 = turn(y, -1), turn(y, 1), turn(y, 2)
    first, second = q == 0, y != z

    def device(yy, zz, xx, qq):
        return (yy, zz * 8 + xx * 2 + qq)

    def on_a(by):
        return device(y, lax.rem(z + q * (by % 4), 4), lax.rem(x + p * (by % 4), 4), q)

    def on_b(by):
        return device(y, lax.rem(z + p * (by % 4), 4), lax.rem(x + q * (by % 4), 4), q)

    def on_y(by):
        return device(turn(y, by), z, x, q)

    mate = device(y, z, x, p)
    mirror = device(z, y, x, q)
    started, count = [], [0]

    def copy(src, dst, to):
        at = count[0]
        count[0] += 1
        return pltpu.make_async_remote_copy(
            src_ref=src, dst_ref=dst, send_sem=send_sem.at[at], recv_sem=recv_sem.at[at],
            device_id=to, device_id_type=MESH,
        )

    def send(src, dst, to):
        c = copy(src, dst, to)
        c.start()
        started.append(c)
        return c

    def left(c):
        c.wait_send()
        started[:] = [other for other in started if other is not c]

    def rows_of(half):
        return pl.ds(pl.multiple_of(half * HALF, HALF), HALF)

    top, bottom = pl.ds(0, PART // 2), pl.ds(PART // 2, PART // 2)

    barrier = pltpu.get_barrier_semaphore()
    others = [mate] + [on(by) for on in (on_a, on_b, on_y) for by in (1, 2, 3)]
    for other in others:
        pl.semaphore_signal(barrier, inc=1, device_id=other, device_id_type=MESH)

    @pl.when(second)
    def _():
        pl.semaphore_signal(barrier, inc=1, device_id=mirror, device_id_type=MESH)

    hid_own = pl.ds(pl.multiple_of(q * HID, HID), HID)
    local_in = pltpu.make_async_copy(w_in, w1.at[:, hid_own], local_sem.at[0])
    local_out = pltpu.make_async_copy(w_out, w2.at[hid_own], local_sem.at[1])
    local_tok = pltpu.make_async_copy(tok_hbm, tok_ref, local_sem.at[2])
    local_cot = pltpu.make_async_copy(cot_hbm, cot_ref, local_sem.at[3])
    local_cot.start()
    local_tok.start()
    local_out.start()
    local_in.start()
    local_cot.wait()
    nat_cot[...] = cot_ref[...].astype(F32).T.astype(BF16)
    local_tok.wait()
    nat_tok[...] = tok_ref[...].astype(F32).T.astype(BF16)

    values = tok_ref[...].astype(F32)
    own_mean = jnp.sum(values, axis=0, keepdims=True) * (1.0 / SHARE)
    own_second = jnp.sum((values - own_mean) ** 2, axis=0, keepdims=True)
    stat[0] = jnp.concatenate([own_mean, own_second, jnp.zeros((6, ROWS), F32)], axis=0)
    gz[z] = jnp.broadcast_to(gain_ref[...].astype(F32).reshape(1, SHARE), (8, SHARE))

    @pl.when(second)
    def _():
        pl.semaphore_wait(barrier, len(others) + 1)

    @pl.when(jnp.logical_not(second))
    def _():
        pl.semaphore_wait(barrier, len(others))

    def joined(own, other):
        return jnp.where(
            first,
            jnp.concatenate([own, other], axis=1),
            jnp.concatenate([other, own], axis=1),
        )

    def mirrored(piece, landing, at_home):
        c = copy(piece, landing, mirror)

        @pl.when(second)
        def _():
            c.start()

        @pl.when(jnp.logical_not(second))
        def _():
            at_home[...] = piece[...]

        return c

    def mirrored_wait(c):
        @pl.when(second)
        def _():
            c.wait_recv()

    def mirrored_sent(c):
        @pl.when(second)
        def _():
            c.wait_send()

    b_there, a_there = p * y + q * x, p * x + q * y

    class Gather:
        def __init__(self, g, part):
            self.g, self.part = g, part

        def at(self, b, a, side=None):
            rows = {None: (0, PART), 0: (0, PART // 2), 1: (PART // 2, PART // 2)}[side]
            return self.g.at[b, a, pl.ds(self.part * PART + rows[0], rows[1])]

        def own(self):
            home = self.at(b0, a0)
            self.a = [send(home, home, on_a(by)) for by in (1, -1, 2)]
            self.b, self.fb = {0: self.both(home)}, []

        def both(self, piece):
            return send(piece, piece, on_b(1)), send(piece, piece, on_b(-1))

        def near(self):
            self.a[0].wait_recv()
            self.b[1] = self.both(self.at(b0, am))
            self.a[1].wait_recv()
            self.b[2] = self.both(self.at(b0, ap))

        def far(self):
            self.a[2].wait_recv()
            self.b[3] = self.both(self.at(b0, a2))

        def onward(self, i):
            a = (a0, am, ap, a2)[i]
            self.b[i][0].wait_recv()
            left = self.at(bm, a, 0)
            up = send(left, left, on_b(1))
            self.b[i][1].wait_recv()
            right = self.at(bp, a, 1)
            down = send(right, right, on_b(-1))
            self.fb.append((up, down))

        def end(self, n):
            for up, down in self.fb:
                up.wait_recv()
                down.wait_recv()
            rows = pl.ds(self.part * PART, PART)
            for j in range(4):
                for s in range(4):
                    to = pl.ds((self.part * 4 + j) * PART, PART)
                    n[to, s * GROUP : (s + 1) * GROUP] = self.g[p * j + q * s, p * s + q * j, rows]

    class RowSum:
        def __init__(self, hf, hb, r1, r2, part):
            self.hf, self.hb = hf.at[part], hb.at[part]
            self.r1, self.r2 = r1.at[part], r2.at[part]

        def compute(self, value):
            hf, hb, r1, r2 = self.hf, self.hb, self.r1, self.r2
            for j in range(4):
                block = value[j * PART : (j + 1) * PART]
                hf[j] = block
                hb[j] = block.astype(BF16)
            self.up1 = send(hb.at[y2, top], r1.at[0], on_y(1))
            self.down1 = send(hb.at[y2, bottom], r1.at[1], on_y(-1))
            self.up2 = send(hb.at[yp, bottom], r2.at[0, bottom], on_y(1))
            self.down2 = send(hb.at[ym, top], r2.at[1, top], on_y(-1))

        def onward(self):
            hf, hb, r1, r2 = self.hf, self.hb, self.r1, self.r2
            self.up1.wait_recv()
            hb[yp, top] = (hf[yp, top] + r1[0].astype(F32)).astype(BF16)
            self.up3 = send(hb.at[yp, top], r2.at[0, top], on_y(1))
            self.down1.wait_recv()
            hb[ym, bottom] = (hf[ym, bottom] + r1[1].astype(F32)).astype(BF16)
            self.down3 = send(hb.at[ym, bottom], r2.at[1, bottom], on_y(-1))

        def end(self):
            for c in (self.up2, self.up3, self.down2, self.down3):
                c.wait_recv()
            return self.hf[y] + self.r2[0].astype(F32) + self.r2[1].astype(F32)

    class RowGather:
        def __init__(self, g, part, block):
            g = self.g = g.at[part]
            g[y] = block
            self.up, self.down = send(g.at[y], g.at[y], on_y(1)), send(g.at[y], g.at[y], on_y(-1))

        def onward(self):
            g = self.g
            self.up.wait_recv()
            self.fup = send(g.at[ym, top], g.at[ym, top], on_y(1))
            self.down.wait_recv()
            self.fdown = send(g.at[yp, bottom], g.at[yp, bottom], on_y(-1))

        def end(self):
            self.fup.wait_recv()
            self.fdown.wait_recv()
            return self.g[...].reshape(4 * PART, PAIR)

    class PlaneSum:
        def __init__(self, pb, r1, r2, s, r4, f, o, part):
            self.pb, self.r1, self.r2, self.s = pb.at[part], r1.at[part], r2.at[part], s.at[part]
            self.r4, self.f, self.o = r4.at[part], f.at[part], o.at[part]

        def compute(self, product):
            pb, r1, r2 = self.pb, self.r1, self.r2
            for wide in range(2):
                value = product(wide * 2 * GROUP, 2 * GROUP)
                for j in range(4):
                    for t in range(2):
                        s = wide * 2 + t
                        pb[p * j + q * s, p * s + q * j] = value[
                            j * PART : (j + 1) * PART, t * GROUP : (t + 1) * GROUP
                        ].astype(BF16)
            self.up1 = send(pb.at[b2, :, top], r1.at[0], on_b(1))
            self.down1 = send(pb.at[b2, :, bottom], r1.at[1], on_b(-1))
            self.up2 = send(pb.at[bp, :, bottom], r2.at[0, :, bottom], on_b(1))
            self.down2 = send(pb.at[bm, :, top], r2.at[1, :, top], on_b(-1))

        def onward(self):
            pb, r1, r2 = self.pb, self.r1, self.r2
            self.up1.wait_recv()
            pb[bp, :, top] = (pb[bp, :, top].astype(F32) + r1[0].astype(F32)).astype(BF16)
            self.up3 = send(pb.at[bp, :, top], r2.at[0, :, top], on_b(1))
            self.down1.wait_recv()
            pb[bm, :, bottom] = (pb[bm, :, bottom].astype(F32) + r1[1].astype(F32)).astype(BF16)
            self.down3 = send(pb.at[bm, :, bottom], r2.at[1, :, bottom], on_b(-1))

        def cross(self):
            pb, r2, s, r4 = self.pb, self.r2, self.s, self.r4
            for c in (self.up2, self.down2, self.up3, self.down3):
                c.wait_recv()

            def summed(a):
                return pb[b0, a].astype(F32) + r2[0, a].astype(F32) + r2[1, a].astype(F32)

            self.a = []
            for slot, (to, by) in enumerate(((a2, 2), (ap, 1), (am, -1))):
                s[to] = summed(to).astype(BF16)
                self.a.append(send(s.at[to], r4.at[slot], on_a(by)))
            self.f[...] = summed(a0)

        def end(self):
            for c in self.a:
                c.wait_recv()
            total = self.f[...] + sum(self.r4[slot].astype(F32) for slot in range(3))
            self.s[a0] = total.astype(BF16)
            self.m = mirrored(self.s.at[a0], self.o, self.o)

    give, keep = rows_of(p), rows_of(q)
    gain_column, moment_columns = [], []
    cot = [Gather(g_cot, m) for m in range(PARTS)]
    tok = [Gather(g_tok, m) for m in range(PARTS)]
    cot_sum = [RowSum(hf_cot, hb_cot, y1_cot, y2_cot, m) for m in range(PARTS)]
    tok_sum = [RowSum(hf_tok, hb_tok, y1_tok, y2_tok, m) for m in range(PARTS)]
    out_sum = [
        PlaneSum(pb_out, r1_out, r2_out, s_out, r4_out, f_out, o_out, m) for m in range(PARTS)
    ]
    gn_sum = [PlaneSum(pb_gn, r1_gn, r2_gn, s_gn, r4_gn, f_gn, o_gn, m) for m in range(PARTS)]
    cot_swaps, tok_swaps, act_gather, gpre_gather, c = {}, {}, {}, {}, {}

    def three(src, buffer, first_slot, on):
        return [send(src, buffer.at[first_slot + by - 1], on(by)) for by in (1, 2, 3)]

    def arrived(copies):
        for one in copies:
            one.wait_recv()

    def on_z(by):
        return device(y, turn(z, by), x, q)

    def on_x(by):
        return device(y, z, turn(x, by), q)

    def start():
        c["mrg_cot"] = send(nat_cot.at[give], mrg_cot, mate)
        c["mrg_tok"] = send(nat_tok.at[give], mrg_tok, mate)
        c["st0"] = send(stat.at[0], stat.at[1], mate)
        c["w2"] = send(w_out, w2.at[hid_own], mate)
        c["w1"] = send(w_in, w1.at[:, hid_own], mate)
        c["gz"] = [send(gz.at[z], gz.at[z], on_z(by)) for by in (1, 2, 3)]

    def cot_merge():
        c["mrg_cot"].wait_recv()
        own_cot[...] = joined(nat_cot[keep].astype(F32), mrg_cot[...].astype(F32)).astype(BF16)

    def cot_swap(m):
        rows = pl.ds(m * PART, PART)
        there, here = g_cot.at[b_there, a_there, rows], g_cot.at[b0, a0, rows]
        cot_swaps[m] = mirrored(own_cot.at[rows], there, here)

    def moments_cores():
        c["st0"].wait_recv()
        stat[2] = merge_moments([stat[0], stat[1]], SHARE)
        c["st1"] = three(stat.at[2], stat, 3, on_a)

    def moments_a():
        arrived(c["st1"])
        stat[6] = merge_moments([stat[2 + by] for by in range(4)], 2 * SHARE)
        c["st2"] = three(stat.at[6], stat, 7, on_b)

    def moments_b():
        arrived(c["st2"])
        moments = merge_moments([stat[6 + by] for by in range(4)], 8 * SHARE)
        inv_std = lax.rsqrt(moments[1:2] * (1.0 / FEATURES) + 1e-06)
        stat[10] = jnp.concatenate([moments[0:1], inv_std, jnp.zeros((6, ROWS), F32)], axis=0)
        c["stM"] = mirrored(stat.at[10], stat.at[11], stat.at[11])

    def own_unit():
        unit[...] = (tok_ref[...].astype(F32) - stat[10, 0:1]) * stat[10, 1:2]
        gain_values = gain_ref[...].astype(F32).reshape(1, SHARE)
        gain_column.append(jnp.broadcast_to(gain_values, (128, SHARE)).T[:, 0:1])

    def tok_merge():
        c["mrg_tok"].wait_recv()
        own_tok[...] = joined(nat_tok[keep].astype(F32), mrg_tok[...].astype(F32)).astype(BF16)

    def tok_swap(m):
        rows = pl.ds(m * PART, PART)
        tok_swaps[m] = mirrored(own_tok.at[rows], raw_tok.at[rows], raw_tok.at[rows])

    def normalise(m):
        if not moment_columns:
            mirrored_wait(c["stM"])
            both = jnp.where(first, stat[11, :, 0:HALF], stat[11, :, HALF:ROWS])
            both = jnp.concatenate([both, jnp.zeros((120, HALF), F32)], axis=0).T
            moment_columns.extend([both[:, 0:1], both[:, 1:2]])
        rows = slice(m * PART, (m + 1) * PART)
        mean, inv_std = (column[rows] for column in moment_columns)
        unit_rows = (raw_tok[rows].astype(F32) - mean) * inv_std
        g_tok[b0, a0, rows] = (unit_rows * gx[x, 0:1]).astype(BF16)

    def gain_z():
        arrived(c["gz"])
        c["gm"] = send(gz.at[y], gz.at[4], mate)

    def gain_cores():
        c["gm"].wait_recv()
        gx[x] = joined(gz[y], gz[4])
        c["gx"] = [send(gx.at[x], gx.at[x], on_x(by)) for by in (1, 2, 3)]

    def gain_x():
        arrived(c["gx"])
        local_in.wait()
        c["w1"].wait_recv()
        gy[0] = sum(
            dot_nn(gx[s].astype(BF16), w1[s * GROUP : (s + 1) * GROUP]) for s in range(4)
        )
        c["gy"] = three(gy.at[0], gy, 1, on_y)

    def part_rows(m):
        return pl.ds(m * 4 * PART, 4 * PART)

    def cot_own(m):
        mirrored_wait(cot_swaps[m])
        cot[m].own()

    def tok_own(m):
        mirrored_wait(tok_swaps[m])
        normalise(m)
        tok[m].own()

    def cot_compute(m):
        if m == FIRST_COT:
            local_out.wait()
            c["w2"].wait_recv()
        cot_sum[m].compute(dot_nt(n_cot[part_rows(m)], w2[...]))

    def tok_compute(m):
        tok_sum[m].compute(dot_nn(n_tok[part_rows(m)], w1[...]))

    def gelu(m):
        hidden_pre = tok_sum[m].end()
        gelu_value, slope[m] = gelu_parts(hidden_pre)
        hidden[m] = hidden_pre
        act_gather[m] = RowGather(act, m, gelu_value.astype(BF16))

    def gradient(m):
        if m == FIRST_PART:
            arrived(c["gy"])
        grad_pre = (cot_sum[m].end() * slope[m]).astype(BF16)
        gpre_gather[m] = RowGather(gpre, m, grad_pre)
        grad_pre = grad_pre.astype(F32)
        gain_row = (gy[0] + gy[1] + gy[2] + gy[3])[0:1]
        one = jnp.sum(grad_pre * gain_row, axis=1, keepdims=True)
        two = jnp.sum(grad_pre * hidden[m], axis=1, keepdims=True)
        lane = lax.broadcasted_iota(jnp.int32, (PART, 128), 1)
        sums[m * PART : (m + 1) * PART] = jnp.where(lane == 0, one, two)

    def means_cores():
        ms[0] = sums[...].T[0:8]
        c["ms0"] = three(ms.at[0], ms, 1, on_a)

    def means_a():
        arrived(c["ms0"])
        ms[4] = ms[0] + ms[1] + ms[2] + ms[3]
        c["ms1"] = three(ms.at[4], ms, 5, on_b)

    def means_b():
        arrived(c["ms1"])
        ms[8] = (ms[4] + ms[5] + ms[6] + ms[7]) * (1.0 / FEATURES)
        c["ms2"] = send(ms.at[8], ms.at[9], mate)

    def out_compute(m):
        block = act_gather[m].end()
        out_sum[m].compute(lambda at, wide: dot_nn(block, w2[:, at : at + wide]))

    def gn_compute(m):
        block = gpre_gather[m].end()
        gn_sum[m].compute(lambda at, wide: dot_nt(block, w1[at : at + wide]))

    def by_hidden(who):
        return pl.ds(pl.multiple_of(who * HID, HID), HID)

    def grad_outer(who, into):
        block = act[:, :, :, by_hidden(who)].reshape(4 * HALF, HID)
        into[...] = dot_tn(block, n_cot[...])

    def grad_inner(who, into):
        block = gpre[:, :, :, by_hidden(who)].reshape(4 * HALF, HID)

        def step(t, _):
            at = pl.ds(pl.multiple_of(t * GROUP, GROUP), GROUP)
            into[at] = dot_tn(n_tok[:, at], block)
            return 0

        lax.fori_loop(0, 4, step, 0)

    def outer_send():
        grad_outer(p, go_send)
        c["go"] = send(go_send, go_recv, mate)

    def inner_send():
        grad_inner(p, gi_send)
        c["gi"] = send(gi_send, gi_recv, mate)

    def outer_add():
        c["go"].wait_recv()
        gouter_ref[...] = go_own[...] + go_recv[...]

    def inner_add():
        c["gi"].wait_recv()
        ginner_ref[...] = gi_own[...] + gi_recv[...]

    def split(sums, o, to_mate, landing):
        for one in sums:
            mirrored_wait(one.m)
        piece = o[...].reshape(HALF, GROUP).astype(F32)
        low, high = piece[:, 0:SHARE], piece[:, SHARE:GROUP]
        to_mate[...] = jnp.where(first, high, low).astype(BF16)
        return jnp.where(first, low, high).astype(BF16), send(to_mate, landing, mate)

    def out_split():
        left(c["mrg_cot"])
        nat_cot[keep], c["out"] = split(out_sum, o_out, c_out, d_out)

    def gn_split():
        left(c["mrg_tok"])
        nat_tok[keep], c["gn"] = split(gn_sum, o_gn, c_gn, d_gn)

    def out_end():
        c["out"].wait_recv()
        nat_cot[give] = d_out[...]
        branch_ref[...] = nat_cot[...].astype(F32).T.astype(BF16)

    def gn_end():
        c["gn"].wait_recv()
        nat_tok[give] = d_gn[...]
        unit_rows = unit[...]
        grad_normed = nat_tok[...].astype(F32).T
        gain_part = jnp.sum(grad_normed * unit_rows, axis=1, keepdims=True)
        ggbuf[0] = jnp.broadcast_to(gain_part, (SHARE, 128)).T[0:8]
        c["gg"] = three(ggbuf.at[0], ggbuf, 1, on_y)
        c["ms2"].wait_recv()
        means = joined(ms[8], ms[9])
        grad_hat = grad_normed * gain_column[0]
        gtok_ref[...] = (
            stat[10, 1:2] * (grad_hat - means[0:1] - unit_rows * means[1:2])
        ).astype(BF16)

    def gain_end():
        arrived(c["gg"])
        ggain_ref[...] = (ggbuf[0] + ggbuf[1] + ggbuf[2] + ggbuf[3])[0:1]

    start()
    cot_merge()
    cot_swap(2)
    cot_swap(0)
    cot_swap(1)
    gain_z()
    moments_cores()
    tok_merge()
    tok_swap(2)
    tok_swap(1)
    tok_swap(0)
    moments_a()
    cot_own(2)
    gain_cores()
    cot_own(0)
    moments_b()
    cot[2].near()
    own_unit()
    cot[2].far()
    cot[2].onward(0)
    gain_x()
    cot[0].near()
    cot[0].onward(0)
    cot[0].far()
    cot[2].onward(1)
    cot[2].onward(2)
    cot[2].onward(3)
    tok_own(2)
    cot[0].onward(1)
    cot[0].onward(2)
    cot[0].onward(3)
    tok_own(0)
    cot[2].end(n_cot)
    cot_compute(2)
    tok[2].far()
    tok[2].near()
    tok[2].onward(0)
    cot[0].end(n_cot)
    cot_compute(0)
    tok[0].near()
    tok[0].far()
    tok[0].onward(0)
    cot_sum[2].onward()
    tok[2].onward(3)
    tok[2].onward(1)
    tok[2].onward(2)
    tok[0].onward(1)
    cot_sum[0].onward()
    tok[0].onward(2)
    tok[0].onward(3)
    tok[2].end(n_tok)
    tok_compute(2)
    tok[0].end(n_tok)
    tok_compute(0)
    cot_own(1)
    tok_sum[2].onward()
    tok_own(1)
    cot[1].near()
    tok_sum[0].onward()
    gelu(2)
    gradient(2)
    cot[1].onward(0)
    tok[1].near()
    tok[1].far()
    tok[1].onward(0)
    cot[1].onward(1)
    cot[1].onward(2)
    gelu(0)
    gradient(0)
    cot[1].far()
    act_gather[2].onward()
    tok[1].onward(1)
    tok[1].onward(2)
    tok[1].onward(3)
    cot[1].onward(3)
    gpre_gather[2].onward()
    tok[1].end(n_tok)
    tok_compute(1)
    act_gather[0].onward()
    cot[1].end(n_cot)
    cot_compute(1)
    gpre_gather[0].onward()
    out_compute(2)
    gn_compute(2)
    tok_sum[1].onward()
    out_compute(0)
    cot_sum[1].onward()
    out_sum[2].onward()
    gn_compute(0)
    gelu(1)
    out_sum[0].onward()
    gradient(1)
    means_cores()
    out_sum[2].cross()
    gn_sum[0].onward()
    gn_sum[2].onward()
    act_gather[1].onward()
    out_sum[0].cross()
    out_sum[2].end()
    gpre_gather[1].onward()
    gn_sum[0].cross()
    gn_sum[2].cross()
    out_compute(1)
    gn_compute(1)
    out_sum[0].end()
    gn_sum[0].end()
    outer_send()
    gn_sum[1].onward()
    gn_sum[2].end()
    out_sum[1].onward()
    inner_send()
    gn_sum[1].cross()
    grad_inner(q, gi_own)
    out_sum[1].cross()
    gn_sum[1].end()
    means_a()
    grad_outer(q, go_own)
    out_sum[1].end()
    means_b()
    gn_split()
    gn_end()
    out_split()
    inner_add()
    out_end()
    outer_add()
    gain_end()

    for one in started:
        one.wait_send()
    swaps = [*cot_swaps.values(), *tok_swaps.values(), c["stM"]]
    for one in (*swaps, *(plane.m for plane in out_sum + gn_sum)):
        mirrored_sent(one)


def scratch():
    def buf(*shape, kind=BF16):
        return pltpu.VMEM(shape, kind)

    def twice(*shape, kind=BF16):
        return [buf(*shape, kind=kind), buf(*shape, kind=kind)]

    return [
        *twice(SHARE, ROWS), buf(CHUNK, PAIR), buf(PAIR, CHUNK),
        buf(SHARE, ROWS, kind=F32), buf(12, 8, ROWS, kind=F32),
        buf(4, 8, SHARE, kind=F32),
        buf(5, 8, SHARE, kind=F32), buf(4, 8, GROUP, kind=F32), buf(4, 8, PAIR, kind=F32),
        buf(PARTS, PART, PAIR, kind=F32), buf(PARTS, PART, PAIR, kind=F32),
        buf(HALF, 128, kind=F32), buf(10, 8, HALF, kind=F32),
        *twice(ROWS, SHARE), *twice(HALF, SHARE), *twice(HALF, GROUP), buf(HALF, GROUP),
        *twice(4, 4, HALF, GROUP), *twice(4 * HALF, CHUNK),
        *twice(PARTS, 4, PART, PAIR, kind=F32), *twice(PARTS, 4, PART, PAIR),
        *twice(PARTS, 2, PART // 2, PAIR), *twice(PARTS, 2, PART, PAIR),
        *twice(PARTS, 4, PART, PAIR),
        *twice(PARTS, 4, 4, PART, GROUP),
        *twice(PARTS, 2, 4, PART // 2, GROUP), *twice(PARTS, 2, 4, PART, GROUP),
        *twice(PARTS, 4, PART, GROUP), *twice(PARTS, 3, PART, GROUP),
        *twice(PARTS, PART, GROUP, kind=F32),
        *twice(PARTS, PART, GROUP), *twice(HALF, SHARE), *twice(HALF, SHARE),
        buf(HID, CHUNK, kind=F32), buf(HID, CHUNK, kind=F32), buf(HID, CHUNK, kind=F32),
        buf(CHUNK, HID, kind=F32), buf(CHUNK, HID, kind=F32), buf(CHUNK, HID, kind=F32),
        pltpu.SemaphoreType.DMA((COPIES,)),
        pltpu.SemaphoreType.DMA((COPIES,)),
        pltpu.SemaphoreType.DMA((4,)),
    ]


def body(tokens, norm_gain, inner_weight, outer_weight, cotangent):
    vmem, anywhere = pl.BlockSpec(memory_space=pltpu.VMEM), pl.BlockSpec(memory_space=pl.ANY)
    shapes = [
        ((SHARE, ROWS), BF16), ((SHARE, ROWS), BF16), ((1, SHARE), F32),
        ((CHUNK, HID), F32), ((HID, CHUNK), F32),
    ]
    branch_out, grad_tokens, grad_gain, grad_inner, grad_outer = pl.pallas_call(
        kernel,
        out_shape=[pltpu.VMEM(shape, kind) for shape, kind in shapes],
        in_specs=[anywhere, vmem, anywhere, anywhere, anywhere],
        out_specs=[vmem] * 5,
        scratch_shapes=scratch(),
        compiler_params=pltpu.CompilerParams(
            collective_id=0, has_side_effects=True, vmem_limit_bytes=VMEM_BYTES
        ),
        name="mlp_block",
    )(tokens.T, norm_gain, inner_weight, outer_weight, cotangent.T)
    return (branch_out.T, grad_tokens.T, grad_gain.reshape(SHARE), grad_inner, grad_outer)


def solution(mesh):
    return jax.shard_map(
        body,
        mesh=mesh,
        in_specs=(P("row", "col"), P("col"), P("row", "col"), P("col", "row"), P("row", "col")),
        out_specs=(P("row", "col"), P("row", "col"), P("col"), P("row", "col"), P("col", "row")),
        check_vma=False,
    )
```
